256 devices in a mesh: section: 32 (over y, z), dp: 8 (over x, core).
Axes of the slice: x: 4, y: 4, z: 8, core: 2. Of those that a mesh axis runs over, the one named last changes fastest.
Arguments:
- stash: bfloat16 [2, 32, 8, 128, 5120], P(None, 'section', None, 'dp'), may hold values from -6 to 6
- cotangent: bfloat16 [8, 128, 5120], P(None, 'dp', 'section'), may hold values from -6 to 6
- a_param: float32 [2, 32, 5120, 128], P(None, 'section', 'dp'), may hold values from -0.078125 to 0.078125
- a_moment: float32 [2, 32, 5120, 128], P(None, 'section', 'dp'), may hold values from -3 to 3
- a_second: float32 [2, 32, 5120, 128], P(None, 'section', 'dp'), may hold values from 0.01 to 1
- b_param: float32 [2, 32, 128, 5120], P(None, 'section', None, 'dp'), may hold values from -0.109375 to 0.109375
- b_moment: float32 [2, 32, 128, 5120], P(None, 'section', None, 'dp'), may hold values from -3 to 3
- b_second: float32 [2, 32, 128, 5120], P(None, 'section', None, 'dp'), may hold values from 0.01 to 1
Outputs:
- new_a_param: float32 [2, 32, 5120, 128], P(None, 'section', 'dp')
- new_a_moment: float32 [2, 32, 5120, 128], P(None, 'section', 'dp')
- new_a_second: float32 [2, 32, 5120, 128], P(None, 'section', 'dp')
- new_b_param: float32 [2, 32, 128, 5120], P(None, 'section', None, 'dp')
- new_b_moment: float32 [2, 32, 128, 5120], P(None, 'section', None, 'dp')
- new_b_second: float32 [2, 32, 128, 5120], P(None, 'section', None, 'dp')
- grad_norm: float32 [], replicated
The draws below stay inside these ranges and needn't reach their ends.
All inputs are finite; a program needn't handle non-finite values.
Results may differ from the reference program's by a relative error of at most 0.013.
Values may be sent and summed in bfloat16 or wider, within the bound.
A program may use at most 128 MiB of HBM per device.

```python
import math
import jax
import jax.numpy as jnp
from jax import lax

D = 5120
RANK = 128
MICRO = 8
TOKENS = 128
ENTRIES = 83886080
N_SECTION = 32


def levels(key, extent, cuts, low, high):
    def one(axis_at, shards_of):
        draws = jax.random.uniform(jax.random.fold_in(jax.random.fold_in(key, 6), axis_at), (shards_of,), jnp.float32, low / len(cuts), high / len(cuts))
        return jnp.repeat(jnp.exp(draws), extent[axis_at] // shards_of).reshape((-1,) + (1,) * (len(extent) - axis_at - 1))

    gain = one(*cuts[0])
    for cut in cuts[1:]:
        gain = gain * one(*cut)
    return gain


def bell_draw(rng, shape, spread, limit, cuts=(), dtype=jnp.bfloat16):
    gain = levels(rng, shape, cuts, -0.22, 0.18) if cuts else 1.0
    values = jax.random.normal(rng, shape, jnp.float32) * spread * gain
    return jnp.minimum(jnp.maximum(values, -limit), limit).astype(dtype)


def setup_inputs(seed: int = 0) -> dict:
    keys = jax.random.split(jax.random.key(seed), 9)
    stash = bell_draw(keys[0], (2, N_SECTION, MICRO, TOKENS, D), 1.0, 6.0, ((1, 32), (3, 8)))
    cotangent = bell_draw(keys[1], (MICRO, TOKENS, D), 1.0, 6.0, ((1, 8), (2, 32)))
    a_param = bell_draw(keys[2], (2, N_SECTION, D, RANK), D ** -0.5, 0.078125, ((1, 32), (2, 8)), jnp.float32)
    a_moment = bell_draw(keys[3], (2, N_SECTION, D, RANK), 0.5, 3.0, ((1, 32), (2, 8)), jnp.float32)
    a_second = jnp.clip(jnp.exp(math.log(1.0) - 4.6051702 * jax.random.uniform(keys[4], (2, N_SECTION, D, RANK), jnp.float32) ** levels(keys[4], (2, N_SECTION, D, RANK), ((1, 32), (2, 8)), -0.2, 0.2)), 0.01, 1.0)
    b_param = bell_draw(keys[5], (2, N_SECTION, RANK, D), (0.2 * RANK ** -0.5), 0.109375, ((1, 32), (3, 8)), jnp.float32)
    b_moment = bell_draw(keys[6], (2, N_SECTION, RANK, D), 0.5, 3.0, ((1, 32), (3, 8)), jnp.float32)
    b_second = jnp.clip(jnp.exp(math.log(1.0) - 4.6051702 * jax.random.uniform(keys[7], (2, N_SECTION, RANK, D), jnp.float32) ** levels(keys[7], (2, N_SECTION, RANK, D), ((1, 32), (3, 8)), -0.2, 0.2)), 0.01, 1.0)
    return {"stash": stash, "cotangent": cotangent, "a_param": a_param, "a_moment": a_moment, "a_second": a_second, "b_param": b_param, "b_moment": b_moment, "b_second": b_second}


beta_one = 0.9
beta_two = 0.95
learning_rate = 0.01
adam_epsilon = 1e-08
norm_epsilon = 1e-06

def normed_parts(inputs):
    values = inputs.astype(jnp.float32)
    inv_rms = lax.rsqrt(lax.optimization_barrier(jnp.mean(values * values, axis=-1, keepdims=True)) + norm_epsilon)
    normed_f = values * inv_rms
    return (inv_rms, normed_f, normed_f.astype(jnp.bfloat16))

def block_backward(inputs, incoming, a_weight, b_weight):
    inv_rms, normed_f, normed = normed_parts(inputs)
    preact = jnp.dot(normed, a_weight, preferred_element_type=jnp.float32)
    gate_sig = jax.nn.sigmoid(preact)
    hidden = (preact * gate_sig).astype(jnp.bfloat16)
    grad_hidden = jnp.dot(incoming, b_weight.T, preferred_element_type=jnp.float32)
    grad_pre = (grad_hidden * gate_sig * (1.0 + preact * (1.0 - gate_sig))).astype(jnp.bfloat16)
    grad_normed = jnp.dot(grad_pre, a_weight.T, preferred_element_type=jnp.float32)
    inner_mean = lax.optimization_barrier(jnp.mean(grad_normed * normed_f, axis=-1, keepdims=True))
    outgoing = (incoming.astype(jnp.float32) + inv_rms * (grad_normed - normed_f * inner_mean)).astype(jnp.bfloat16)
    return (outgoing, normed, hidden, grad_pre)

def adam_update(param, moment, second, grad, clip_factor):
    scaled = clip_factor * grad
    moment_new = beta_one * moment + (1.0 - beta_one) * scaled
    second_new = beta_two * second + (1.0 - beta_two) * scaled * scaled
    param_new = param - learning_rate * moment_new / (jnp.sqrt(second_new) + adam_epsilon)
    return (param_new, moment_new, second_new)

def reference(stash, cotangent, a_param, a_moment, a_second, b_param, b_moment, b_second):
    a_bf = a_param.astype(jnp.bfloat16)
    b_bf = b_param.astype(jnp.bfloat16)
    a_order = jnp.concatenate([a_bf[1], a_bf[0][::-1]], axis=0)
    b_order = jnp.concatenate([b_bf[1], b_bf[0][::-1]], axis=0)
    x_order = jnp.concatenate([stash[1], stash[0][::-1]], axis=0)
    row_count = MICRO * TOKENS

    def chain_step(incoming, pieces):
        inputs, a_weight, b_weight = pieces
        outgoing, normed, hidden, grad_pre = block_backward(inputs.reshape(row_count, D), incoming, a_weight, b_weight)
        grad_a = jnp.dot(normed.T, grad_pre, preferred_element_type=jnp.float32)
        grad_b = jnp.dot(hidden.T, incoming, preferred_element_type=jnp.float32)
        return (outgoing, (grad_a, grad_b))
    final_delta, (grads_a, grads_b) = lax.scan(chain_step, cotangent.reshape(row_count, D), (x_order, a_order, b_order))
    grad_a_all = jnp.stack([grads_a[N_SECTION:][::-1], grads_a[:N_SECTION]], axis=0)
    grad_b_all = jnp.stack([grads_b[N_SECTION:][::-1], grads_b[:N_SECTION]], axis=0)
    square_total = jnp.sum(grad_a_all * grad_a_all) + jnp.sum(grad_b_all * grad_b_all)
    grad_norm = jnp.sqrt(square_total)
    clip_factor = jnp.minimum(1.0, 0.5 * math.sqrt(ENTRIES) / grad_norm)
    a_new, a_moment_new, a_second_new = adam_update(a_param, a_moment, a_second, grad_a_all, clip_factor)
    b_new, b_moment_new, b_second_new = adam_update(b_param, b_moment, b_second, grad_b_all, clip_factor)
    return (a_new, a_moment_new, a_second_new, b_new, b_moment_new, b_second_new, grad_norm)
```

```python
import functools
import math

import jax
import jax.numpy as jnp
from jax import lax
from jax.experimental import pallas as pl
from jax.experimental.pallas import tpu as pltpu
from jax.sharding import PartitionSpec as P

beta_one = 0.9
beta_two = 0.95
learning_rate = 0.01
adam_epsilon = 1e-08
norm_epsilon = 1e-06

MESH = pl.DeviceIdType.MESH
F32 = jnp.float32
BF16 = jnp.bfloat16

N_SECTION = 32
N_Z = 8
N_X = 4
N_DP = 8
D = 5120
RANK = 128
MICRO = 8
TILE = 16
SHARD = D // N_DP
FOLD = 4
ROWS = TILE // FOLD
CHUNKS = MICRO * FOLD
WIDE = D // FOLD
PER_PART = WIDE // SHARD
LATE = 16
LAG = 5

NT = (((1,), (1,)), ((), ()))
TN = (((0,), (0,)), ((), ()))


def row_group():
    return lax.broadcasted_iota(jnp.int32, (TILE, RANK), 0) // ROWS


def spread(value):
    step = TILE // 2
    while step >= ROWS:
        value = value + pltpu.roll(value, step, 0)
        step //= 2
    return value


def diagonal(value, group):
    return jnp.concatenate([jnp.where(group == q, value, 0.0) for q in range(FOLD)], axis=1)


def chain_kernel(
    stash, cot, a_param, b_param,
    grad_a, grad_b, total,
    w_b, w_a, x_fold, d_in, d_out, gate, slope, p_diag, h_diag, window,
    keep, pair_out, pair_in, ring_out, ring_in, norm_out, norm_in, lane_out, lane_in, tot_in,
    gat_s, gat_r, ch_s, ch_r, cot_s, cot_r, pair_s, pair_r, ring_s, ring_r, nrm_s, nrm_r, lan_s, lan_r, tot_s, tot_r,
):
    s = lax.axis_index("section")
    d = lax.axis_index("dp")
    x = d // 2
    c = d % 2
    right = lax.rem(x + 1, N_X)
    left = lax.rem(x + N_X - 1, N_X)
    far = lax.rem(x + 2, N_X)
    sib = (s, 2 * x + 1 - c)
    dev_right = (s, 2 * right + c)
    dev_left = (s, 2 * left + c)
    first = s == 0
    last = s == N_SECTION - 1
    down = (jnp.minimum(s + 1, N_SECTION - 1), d)
    up = (jnp.maximum(s - 1, 0), d)
    home = (0, d)
    group = row_group()

    def copy(src, dst, ssem, rsem, dev):
        return pltpu.make_async_remote_copy(
            src_ref=src, dst_ref=dst, send_sem=ssem, recv_sem=rsem, device_id=dev, device_id_type=MESH
        )

    bar = pltpu.get_barrier_semaphore()

    def hello(dev):
        pl.semaphore_signal(bar, inc=1, device_id=dev, device_id_type=MESH)

    hello(sib)
    hello(dev_right)
    hello(dev_left)

    @pl.when(s > 0)
    def _():
        hello(up)
        hello(home)

    @pl.when(s < N_SECTION - 1)
    def _():
        hello(down)

    @pl.when(first)
    def _():
        def lanes(i, carry):
            hello((i, d))
            return carry

        lax.fori_loop(1, N_SECTION, lanes, 0)

        def peers(i, carry):
            hello((0, lax.rem(d + i, N_DP)))
            return carry

        lax.fori_loop(1, N_DP, peers, 0)

    def b_slice(u, e):
        row = pl.multiple_of((e % PER_PART) * SHARD, SHARD)
        col = pl.multiple_of((e // PER_PART) * RANK, RANK)
        return w_b.at[u, pl.ds(row, SHARD), pl.ds(col, RANK)]

    def a_slice(u, e):
        row = pl.multiple_of((e // PER_PART) * RANK, RANK)
        col = pl.multiple_of((e % PER_PART) * SHARD, SHARD)
        return w_a.at[u, pl.ds(row, RANK), pl.ds(col, SHARD)]

    def own_weights(u):
        b_slice(u, d)[...] = b_param[u].T.astype(BF16)
        a_slice(u, d)[...] = a_param[u].T.astype(BF16)

    def refold(get, u, dst, m):
        for at in range(0, WIDE, RANK):
            parts = [get(q, at) for q in range(FOLD)]
            outs = [None] * FOLD
            for q in range(FOLD):
                for j in range(FOLD):
                    turn = (ROWS * (q - j)) % TILE
                    moved = parts[q] if turn == 0 else pltpu.roll(parts[q], turn, 0)
                    outs[j] = moved if q == 0 else jnp.where(group == q, moved, outs[j])
            for j in range(FOLD):
                dst[u, m * FOLD + j, :, at : at + RANK] = outs[j].astype(BF16)

    def fold_stash(u):
        def micro(m, carry):
            refold(lambda q, at: stash[u, m, :, q * WIDE + at : q * WIDE + at + RANK].astype(F32), u, x_fold, m)
            return carry

        lax.fori_loop(0, MICRO, micro, 0)

    own_weights(1)
    own_weights(0)
    fold_stash(1)

    pl.semaphore_wait(
        bar,
        3 + (s > 0).astype(jnp.int32) + (s < N_SECTION - 1).astype(jnp.int32) + jnp.where(first, N_SECTION + N_DP - 2, 1),
    )

    @pl.when(s > 0)
    def _():
        copy(cot, window.at[s], cot_s, cot_r.at[s], home).start()

    def gather_copy(u, slot, xs, cs, kind, dev):
        e = 2 * xs + cs
        ref = b_slice(u, e) if kind == 0 else a_slice(u, e)
        return copy(ref, ref, gat_s.at[u, slot], gat_r.at[u, slot], dev)

    def gather_sends(u):
        return [
            gather_copy(u, 0, x, c, 0, dev_right),
            gather_copy(u, 1, x, c, 1, dev_right),
            gather_copy(u, 2, x, c, 0, dev_left),
            gather_copy(u, 3, x, c, 1, dev_left),
            gather_copy(u, 4, left, c, 0, dev_right),
            gather_copy(u, 5, right, c, 1, dev_left),
        ] + [
            gather_copy(u, 6 + 2 * i + kind, xs, c, kind, sib)
            for i, xs in enumerate((x, left, right, far))
            for kind in (0, 1)
        ]

    def gather_recvs(u):
        return [
            gather_copy(u, 0, left, c, 0, dev_left),
            gather_copy(u, 1, left, c, 1, dev_left),
            gather_copy(u, 2, right, c, 0, dev_right),
            gather_copy(u, 3, right, c, 1, dev_right),
            gather_copy(u, 4, far, c, 0, dev_left),
            gather_copy(u, 5, far, c, 1, dev_right),
        ] + [
            gather_copy(u, 6 + 2 * i + kind, xs, 1 - c, kind, sib)
            for i, xs in enumerate((x, left, right, far))
            for kind in (0, 1)
        ]

    def gather(u):
        out, arr = gather_sends(u), gather_recvs(u)
        out[0].start()
        out[3].start()
        out[1].start()
        out[2].start()
        out[6].start()
        out[7].start()
        arr[0].wait_recv()
        out[4].start()
        out[8].start()
        arr[3].wait_recv()
        out[5].start()
        out[11].start()
        arr[1].wait_recv()
        out[9].start()
        arr[2].wait_recv()
        out[10].start()
        arr[4].wait_recv()
        out[12].start()
        arr[5].wait_recv()
        out[13].start()
        for i in range(6, 14):
            arr[i].wait_recv()

    def gates(u):
        flat = MICRO * TILE
        pre = jnp.zeros((flat, RANK), F32)
        squares = jnp.zeros((flat, 1), F32)
        for e in range(N_DP):
            part = stash[u, :, :, e * SHARD : (e + 1) * SHARD].reshape(flat, SHARD)
            wide = part.astype(F32)
            squares = squares + jnp.sum(wide * wide, axis=1, keepdims=True)
            q, off = e // PER_PART, (e % PER_PART) * SHARD
            pre = pre + lax.dot_general(
                part, w_a[u, q * RANK : (q + 1) * RANK, off : off + SHARD], NT, preferred_element_type=F32
            )
        inv = lax.rsqrt(squares * (1.0 / D) + norm_epsilon)
        pre = pre * inv
        sig = 1.0 / (1.0 + jnp.exp(-pre))
        hidden = pre * sig
        turn = sig * (1.0 + pre * (1.0 - sig)) * inv
        lean = pre * inv * (1.0 / D)
        for m in range(MICRO):
            for j in range(FOLD):
                here = m * FOLD + j
                rows = slice(m * TILE, (m + 1) * TILE)
                gate[u, here] = spread(jnp.where(group == j, turn[rows], 0.0))
                slope[u, here] = spread(jnp.where(group == j, lean[rows], 0.0))
                h_diag[u, here] = diagonal(spread(jnp.where(group == j, hidden[rows], 0.0)), group).astype(BF16)

    def prepare(u):
        gather(u)
        gates(u)

    def chain_copy(u, k, dev):
        return copy(d_out.at[u, k], d_in.at[u, k], ch_s.at[u, k], ch_r.at[u, k], dev)

    def block(u, k):
        incoming = d_in[u, k]
        wide = jnp.dot(incoming, w_b[u], preferred_element_type=F32)
        picked = jnp.where(group == 0, wide[:, :RANK], 0.0)
        for q in range(1, FOLD):
            picked = jnp.where(group == q, wide[:, q * RANK : (q + 1) * RANK], picked)
        grad_hidden = spread(picked)
        grad_pre = (grad_hidden * gate[u, k]).astype(BF16).astype(F32)
        shift = jnp.sum(grad_pre * slope[u, k], axis=1, keepdims=True)
        diag = diagonal(grad_pre, group).astype(BF16)
        p_diag[u, k] = diag
        back = jnp.dot(diag, w_a[u], preferred_element_type=F32)
        return (incoming.astype(F32) + back - x_fold[u, k].astype(F32) * shift).astype(BF16)

    def upper(k):
        @pl.when(s > 0)
        def _():
            chain_copy(1, k, up).wait_recv()

        out = block(1, k)

        @pl.when(last)
        def _():
            d_in[0, k] = out

        @pl.when(s < N_SECTION - 1)
        def _():
            d_out[1, k] = out
            chain_copy(1, k, down).start()

    def lower(k):
        @pl.when(s < N_SECTION - 1)
        def _():
            chain_copy(0, k, down).wait_recv()

        out = block(0, k)

        @pl.when(s > 0)
        def _():
            d_out[0, k] = out
            chain_copy(0, k, up).start()

    def partial(u, kind, e):
        q = e // PER_PART
        col = pl.multiple_of((e % PER_PART) * SHARD, SHARD)
        left_side = h_diag if kind == 0 else p_diag
        right_side = d_in if kind == 0 else x_fold
        rows = CHUNKS * TILE
        lane = pl.multiple_of(q * RANK, RANK)
        lhs = left_side[u, :, :, pl.ds(lane, RANK)].reshape(rows, RANK)
        rhs = right_side[u, :, :, pl.ds(col, SHARD)].reshape(rows, SHARD)
        return lax.dot_general(lhs, rhs, TN, preferred_element_type=F32)

    def pair_copy(u, kind):
        return copy(pair_out.at[u, kind], pair_in.at[u, kind], pair_s.at[u, kind], pair_r.at[u, kind], sib)

    def ring_copy(u, kind, slot, dev):
        return copy(
            ring_out.at[u, kind, slot], ring_in.at[u, kind, slot], ring_s.at[u, kind, slot], ring_r.at[u, kind, slot], dev
        )

    def gradients(u):
        for kind in (0, 1):
            def theirs(i, carry):
                pair_out[u, kind, i] = partial(u, kind, 2 * i + 1 - c).astype(BF16)
                return carry

            lax.fori_loop(0, N_X, theirs, 0)
            pair_copy(u, kind).start()
        for kind in (0, 1):
            def ours(i, carry):
                keep[u, kind, i] = partial(u, kind, 2 * i + c)
                return carry

            lax.fori_loop(0, N_X, ours, 0)
        ways = ((dev_right, right, dev_left, left), (dev_left, left, dev_right, right))
        for kind in (0, 1):
            ahead, ahead_x, behind, behind_x = ways[kind]
            pair_copy(u, kind).wait_recv()
            keep[u, kind] = keep[u, kind] + pair_in[u, kind].astype(F32)
            ring_out[u, kind, 0] = keep[u, kind, far].astype(BF16)
            ring_copy(u, kind, 0, ahead).start()
            ring_out[u, kind, 1] = keep[u, kind, behind_x].astype(BF16)
            ring_copy(u, kind, 1, behind).start()
        for kind in (0, 1):
            ahead, ahead_x, behind, behind_x = ways[kind]
            ring_copy(u, kind, 0, behind).wait_recv()
            ring_out[u, kind, 2] = (keep[u, kind, ahead_x] + ring_in[u, kind, 0].astype(F32)).astype(BF16)
            ring_copy(u, kind, 2, ahead).start()

    def collect(u):
        ways = ((dev_right, dev_left), (dev_left, dev_right))
        squares = jnp.zeros((1, 1), F32)
        for kind in (0, 1):
            ahead, behind = ways[kind]
            ring_copy(u, kind, 1, ahead).wait_recv()
            ring_copy(u, kind, 2, behind).wait_recv()
            grad = keep[u, kind, x] + ring_in[u, kind, 1].astype(F32) + ring_in[u, kind, 2].astype(F32)
            squares = squares + jnp.sum(jnp.sum(grad * grad, axis=0, keepdims=True), axis=1, keepdims=True)
            if kind == 0:
                grad_b[u] = grad
            else:
                grad_a[u] = grad.T
        return squares

    prepare(1)

    @pl.when(first)
    def _():
        window[0] = cot[...]

        def arrive(i, carry):
            copy(cot, window.at[i], cot_s, cot_r.at[i], sib).wait_recv()
            return carry

        lax.fori_loop(1, N_SECTION, arrive, 0)

        def tile(q, at, m):
            column = (q * WIDE + at) // RANK
            base, place = column // 5 * 4, column % 5
            value = None
            if place < 4:
                value = window[base + place, pl.ds(pl.multiple_of(m * TILE, TILE), TILE), :RANK].astype(F32)
            if place > 0:
                other = window[base + place - 1, pl.ds(pl.multiple_of(m * TILE, TILE), TILE), RANK:].astype(F32)
                value = other if value is None else value + other
            return value

        def micro(m, carry):
            refold(lambda q, at: tile(q, at, m), 1, d_in, m)
            return carry

        lax.fori_loop(0, MICRO, micro, 0)

    @pl.when(s >= LATE)
    def _():
        fold_stash(0)
        prepare(0)

    lag = jnp.where(s < LATE, CHUNKS, jnp.minimum(CHUNKS, LAG * (N_SECTION - 1 - s)))

    def tick(t, carry):
        upper(t)

        @pl.when(t >= lag)
        def _():
            lower(t - lag)

        return carry

    lax.fori_loop(0, CHUNKS, tick, 0)

    @pl.when(s < LATE)
    def _():
        fold_stash(0)
        prepare(0)
        gradients(1)

    def rest(k, carry):
        lower(k)
        return carry

    lax.fori_loop(CHUNKS - lag, CHUNKS, rest, 0)

    @pl.when(s >= LATE)
    def _():
        gradients(1)

    gradients(0)
    squares = collect(1) + collect(0)

    mine = jnp.broadcast_to(squares, (8, 128))

    @pl.when(s > 0)
    def _():
        norm_out[...] = mine
        up_copy = copy(norm_out, norm_in.at[s], nrm_s, nrm_r.at[s], home)
        up_copy.start()
        back = copy(lane_out, tot_in, lan_s.at[0], tot_r, home)
        back.wait_recv()
        total[...] = tot_in[...]
        up_copy.wait_send()

    @pl.when(first)
    def _():
        norm_in[0] = mine

        def arrive(i, carry):
            copy(norm_out, norm_in.at[i], nrm_s, nrm_r.at[i], sib).wait_recv()
            return carry

        lax.fori_loop(1, N_SECTION, arrive, 0)
        lane_out[...] = jnp.sum(norm_in[...], axis=0)

        def share(i):
            return copy(lane_out, lane_in.at[i], lan_s.at[i], lan_r.at[i], (0, lax.rem(d + i, N_DP)))

        for i in range(1, N_DP):
            share(i).start()
        for i in range(1, N_DP):
            share(i).wait_recv()
        lane_in[0] = lane_out[...]
        value = jnp.sum(lane_in[...], axis=0)
        total[...] = value
        norm_out[...] = value

        def send(i, carry):
            copy(norm_out, tot_in, tot_s.at[i], tot_r, (i, d)).start()
            return carry

        lax.fori_loop(1, N_SECTION, send, 0)

        def sent(i, carry):
            copy(norm_out, tot_in, tot_s.at[i], tot_r, (i, d)).wait_send()
            return carry

        lax.fori_loop(1, N_SECTION, sent, 0)
        for i in range(1, N_DP):
            share(i).wait_send()

    @pl.when(s > 0)
    def _():
        copy(cot, window.at[s], cot_s, cot_r.at[s], home).wait_send()

    for u in (0, 1):
        for one in gather_sends(u):
            one.wait_send()
        for kind in (0, 1):
            pair_copy(u, kind).wait_send()
            for slot in range(3):
                ring_copy(u, kind, slot, sib).wait_send()

    @pl.when(s < N_SECTION - 1)
    def _():
        def sent(k, carry):
            chain_copy(1, k, down).wait_send()
            return carry

        lax.fori_loop(0, CHUNKS, sent, 0)

    @pl.when(s > 0)
    def _():
        def sent(k, carry):
            chain_copy(0, k, up).wait_send()
            return carry

        lax.fori_loop(0, CHUNKS, sent, 0)


def chain(stash, cot, a_param, b_param):
    dma = pltpu.SemaphoreType.DMA
    vmem = pl.BlockSpec(memory_space=pltpu.VMEM)
    part = (2, 2, N_X, RANK, SHARD)
    return pl.pallas_call(
        chain_kernel,
        name="chain",
        out_shape=(
            jax.ShapeDtypeStruct((2, SHARD, RANK), F32),
            jax.ShapeDtypeStruct((2, RANK, SHARD), F32),
            jax.ShapeDtypeStruct((8, 128), F32),
        ),
        in_specs=[vmem] * 4,
        out_specs=(vmem,) * 3,
        scratch_shapes=[
            pltpu.VMEM((2, WIDE, FOLD * RANK), BF16),
            pltpu.VMEM((2, FOLD * RANK, WIDE), BF16),
            pltpu.VMEM((2, CHUNKS, TILE, WIDE), BF16),
            pltpu.VMEM((2, CHUNKS, TILE, WIDE), BF16),
            pltpu.VMEM((2, CHUNKS, TILE, WIDE), BF16),
            pltpu.VMEM((2, CHUNKS, TILE, RANK), F32),
            pltpu.VMEM((2, CHUNKS, TILE, RANK), F32),
            pltpu.VMEM((2, CHUNKS, TILE, FOLD * RANK), BF16),
            pltpu.VMEM((2, CHUNKS, TILE, FOLD * RANK), BF16),
            pltpu.VMEM((N_SECTION, MICRO * TILE, 2 * RANK), BF16),
            pltpu.VMEM(part, F32),
            pltpu.VMEM(part, BF16),
            pltpu.VMEM(part, BF16),
            pltpu.VMEM((2, 2, 3, RANK, SHARD), BF16),
            pltpu.VMEM((2, 2, 3, RANK, SHARD), BF16),
            pltpu.VMEM((8, 128), F32),
            pltpu.VMEM((N_SECTION, 8, 128), F32),
            pltpu.VMEM((8, 128), F32),
            pltpu.VMEM((N_DP, 8, 128), F32),
            pltpu.VMEM((8, 128), F32),
            dma((2, 14)), dma((2, 14)),
            dma((2, CHUNKS)), dma((2, CHUNKS)),
            dma, dma((N_SECTION,)),
            dma((2, 2)), dma((2, 2)),
            dma((2, 2, 3)), dma((2, 2, 3)),
            dma, dma((N_SECTION,)),
            dma((N_DP,)), dma((N_DP,)),
            dma((N_SECTION,)), dma,
        ],
        compiler_params=pltpu.CompilerParams(collective_id=0, has_side_effects=True, vmem_limit_bytes=58 << 20),
    )(stash, cot, a_param, b_param)


def adam_update(param, moment, second, grad, clip_factor):
    scaled = clip_factor * grad
    moment_new = beta_one * moment + (1.0 - beta_one) * scaled
    second_new = beta_two * second + (1.0 - beta_two) * scaled * scaled
    param_new = param - learning_rate * moment_new / (jnp.sqrt(second_new) + adam_epsilon)
    return (param_new, moment_new, second_new)


def shards(stash, cotangent, a_param, a_moment, a_second, b_param, b_moment, b_second):
    position = lax.axis_index("section")
    flat = cotangent.reshape(MICRO * TILE, D // N_SECTION)
    cot = lax.dynamic_update_slice(
        jnp.zeros((MICRO * TILE, 2 * RANK), BF16), flat, (0, 32 * lax.rem(position, 4))
    )
    grad_a, grad_b, total = chain(stash[:, 0], cot, a_param[:, 0], b_param[:, 0])
    grad_norm = jnp.sqrt(total[0, 0])
    entries = 4 * N_SECTION * D * RANK
    clip_factor = jnp.minimum(1.0, 0.5 * math.sqrt(entries) / grad_norm)
    a_new, a_moment_new, a_second_new = adam_update(a_param, a_moment, a_second, grad_a[:, None], clip_factor)
    b_new, b_moment_new, b_second_new = adam_update(b_param, b_moment, b_second, grad_b[:, None], clip_factor)
    return (a_new, a_moment_new, a_second_new, b_new, b_moment_new, b_second_new, grad_norm)


def solution(mesh):
    return jax.shard_map(
        shards,
        mesh=mesh,
        in_specs=(
            P(None, "section", None, "dp", None),
            P(None, "dp", "section"),
            P(None, "section", "dp", None),
            P(None, "section", "dp", None),
            P(None, "section", "dp", None),
            P(None, "section", None, "dp"),
            P(None, "section", None, "dp"),
            P(None, "section", None, "dp"),
        ),
        out_specs=(
            P(None, "section", "dp", None),
            P(None, "section", "dp", None),
            P(None, "section", "dp", None),
            P(None, "section", None, "dp"),
            P(None, "section", None, "dp"),
            P(None, "section", None, "dp"),
            P(),
        ),
        check_vma=False,
    )
```

```python
import functools
import math

import jax
import jax.numpy as jnp
from jax import lax
from jax.experimental import pallas as pl
from jax.experimental.pallas import tpu as pltpu
from jax.sharding import PartitionSpec as P

beta_one = 0.9
beta_two = 0.95
learning_rate = 0.01
adam_epsilon = 1e-08
norm_epsilon = 1e-06

MESH = pl.DeviceIdType.MESH
F32 = jnp.float32
BF16 = jnp.bfloat16

N_SECTION = 32
N_Z = 8
N_X = 4
N_DP = 8
D = 5120
RANK = 128
MICRO = 8
TILE = 16
SHARD = D // N_DP
FOLD = 4
ROWS = TILE // FOLD
CHUNKS = MICRO * FOLD
WIDE = D // FOLD
PER_PART = WIDE // SHARD
TEAM = 4
TEAMS = N_SECTION // TEAM
SHARE = CHUNKS // TEAM
HALF = SHARE // 2
INPUTS, GATES, OPEN, LATE = 1, 2, 3, 7
BACK = 6
EARLY = 3
LAG = 5

NT = (((1,), (1,)), ((), ()))
TN = (((0,), (0,)), ((), ()))


def row_group():
    return lax.broadcasted_iota(jnp.int32, (TILE, RANK), 0) // ROWS


def spread(value):
    step = TILE // 2
    while step >= ROWS:
        value = value + pltpu.roll(value, step, 0)
        step //= 2
    return value


def diagonal(value, group):
    return jnp.concatenate([jnp.where(group == q, value, 0.0) for q in range(FOLD)], axis=1)


def chain_kernel(
    stash, cot, a_param, b_param,
    grad_a, grad_b, total,
    w_b, w_a, x_fold, gates_own, hid, d_in, p_in, x_slot, gates_slot, d_slot, p_slot, d_out, window, mask,
    keep, pair_out, pair_in, ring_out, ring_in, norm_out, norm_in, lane_out, lane_in, tot_in,
    zw_s, zw_r, gat_s, gat_r, dx_s, dx_r, dg_s, dg_r, rd_s, rd_r, rp_s, rp_r, ch_s, ch_r, cot_s, cot_r,
    pair_s, pair_r, ring_s, ring_r, nrm_s, nrm_r, lan_s, lan_r, tot_s, tot_r,
):
    s = lax.axis_index("section")
    d = lax.axis_index("dp")
    x = d // 2
    c = d % 2
    right = lax.rem(x + 1, N_X)
    left = lax.rem(x + N_X - 1, N_X)
    far = lax.rem(x + 2, N_X)
    sib = (s, 2 * x + 1 - c)
    dev_right = (s, 2 * right + c)
    dev_left = (s, 2 * left + c)
    team = s // TEAM
    own = s % TEAM
    odd = team % 2
    base = team * TEAM

    def slot_of(i):
        return i + odd * (TEAM - 1 - 2 * i)

    slot = slot_of(own)
    mine = slot * SHARE
    first = team == 0
    last = team == TEAMS - 1
    down = (jnp.minimum(base + TEAM + TEAM - 1 - own, N_SECTION - 1), d)
    up = (jnp.maximum(base - 1 - own, 0), d)
    home = (0, d)
    group = row_group()

    def mate(j):
        return lax.rem(own + j, TEAM)

    def copy(src, dst, ssem, rsem, dev):
        return pltpu.make_async_remote_copy(
            src_ref=src, dst_ref=dst, send_sem=ssem, recv_sem=rsem, device_id=dev, device_id_type=MESH
        )

    def repeat(low, high, body):
        def step(i, carry):
            body(i)
            return carry

        lax.fori_loop(low, high, step, 0)

    bar = pltpu.get_barrier_semaphore()

    def hello(dev):
        pl.semaphore_signal(bar, inc=1, device_id=dev, device_id_type=MESH)

    hello(sib)
    hello(dev_right)
    hello(dev_left)
    for j in range(1, TEAM):
        hello((base + mate(j), d))

    @pl.when(team > 0)
    def _():
        hello(up)

    @pl.when(team < TEAMS - 1)
    def _():
        hello(down)

    @pl.when(s > 0)
    def _():
        hello(home)

    @pl.when(first)
    def _():
        repeat(1, N_SECTION, lambda i: hello((lax.rem(s + i, N_SECTION), d)))

    @pl.when(s == 0)
    def _():
        repeat(1, N_DP, lambda i: hello((0, lax.rem(d + i, N_DP))))

    def b_slice(u, i, e):
        row = pl.multiple_of((e % PER_PART) * SHARD, SHARD)
        col = pl.multiple_of((e // PER_PART) * RANK, RANK)
        return w_b.at[u, i, pl.ds(row, SHARD), pl.ds(col, RANK)]

    def a_slice(u, i, e):
        row = pl.multiple_of((e // PER_PART) * RANK, RANK)
        col = pl.multiple_of((e % PER_PART) * SHARD, SHARD)
        return w_a.at[u, i, pl.ds(row, RANK), pl.ds(col, SHARD)]

    def piece(u, i, e, kind):
        return b_slice(u, i, e) if kind == 0 else a_slice(u, i, e)

    def own_weights(u):
        b_slice(u, own, d)[...] = b_param[u].T.astype(BF16)
        a_slice(u, own, d)[...] = a_param[u].T.astype(BF16)

    def refold(get, put):
        for at in range(0, WIDE, RANK):
            parts = [get(q, at) for q in range(FOLD)]
            outs = [None] * FOLD
            for q in range(FOLD):
                for j in range(FOLD):
                    turn = (ROWS * (q - j)) % TILE
                    moved = parts[q] if turn == 0 else pltpu.roll(parts[q], turn, 0)
                    outs[j] = moved if q == 0 else jnp.where(group == q, moved, outs[j])
            for j in range(FOLD):
                put(j, at, outs[j].astype(BF16))

    def fold_stash(u):
        def micro(m):
            def put(j, at, value):
                x_fold[u, m * FOLD + j, :, at : at + RANK] = value

            refold(lambda q, at: stash[u, m, :, q * WIDE + at : q * WIDE + at + RANK].astype(F32), put)

        repeat(0, MICRO, micro)

    own_weights(1)
    own_weights(0)
    for q in range(FOLD):
        mask[q] = jnp.where(group == q, 1.0, 0.0).astype(BF16)

    pl.semaphore_wait(
        bar,
        6
        + (team > 0).astype(jnp.int32)
        + (team < TEAMS - 1).astype(jnp.int32)
        + jnp.where(first, TEAM - 1, TEAM)
        + jnp.where(s == 0, N_SECTION + N_DP - 2, 0),
    )

    def team_weights(u, j, kind):
        i = mate(j)
        ref = piece(u, own, d, kind)
        return copy(ref, ref, zw_s.at[u, kind, i], zw_r.at[u, kind, own], (base + i, d))

    def team_weights_in(u, j, kind):
        i = mate(j)
        ref = piece(u, i, d, kind)
        return copy(ref, ref, zw_s.at[u, kind, i], zw_r.at[u, kind, i], (base + i, d))

    def share_x(u, j):
        i = mate(j)
        src = x_fold.at[u, pl.ds(slot_of(i) * SHARE, SHARE)]
        return copy(src, x_slot.at[u, own], dx_s.at[u, i], dx_r.at[u, own], (base + i, d))

    def share_x_in(u, j):
        i = mate(j)
        src = x_fold.at[u, pl.ds(mine, SHARE)]
        return copy(src, x_slot.at[u, i], dx_s.at[u, i], dx_r.at[u, i], (base + i, d))

    def share_gates(u, j):
        i = mate(j)
        src = gates_own.at[u, pl.ds(slot_of(i) * SHARE, SHARE)]
        return copy(src, gates_slot.at[u, own], dg_s.at[u, i], dg_r.at[u, own], (base + i, d))

    def share_gates_in(u, j):
        i = mate(j)
        src = gates_own.at[u, pl.ds(mine, SHARE)]
        return copy(src, gates_slot.at[u, i], dg_s.at[u, i], dg_r.at[u, i], (base + i, d))

    def back_d(u, j, h):
        i = mate(j)
        src = d_slot.at[u, i, pl.ds(h * HALF, HALF)]
        dst = d_in.at[u, pl.ds(mine + h * HALF, HALF)]
        return copy(src, dst, rd_s.at[u, i, h], rd_r.at[u, own, h], (base + i, d))

    def back_d_in(u, j, h):
        i = mate(j)
        src = d_slot.at[u, i, pl.ds(h * HALF, HALF)]
        dst = d_in.at[u, pl.ds(slot_of(i) * SHARE + h * HALF, HALF)]
        return copy(src, dst, rd_s.at[u, i, h], rd_r.at[u, i, h], (base + i, d))

    def back_p(u, j, h):
        i = mate(j)
        src = p_slot.at[u, i, pl.ds(h * HALF, HALF)]
        dst = p_in.at[u, pl.ds(mine + h * HALF, HALF)]
        return copy(src, dst, rp_s.at[u, i, h], rp_r.at[u, own, h], (base + i, d))

    def back_p_in(u, j, h):
        i = mate(j)
        src = p_slot.at[u, i, pl.ds(h * HALF, HALF)]
        dst = p_in.at[u, pl.ds(slot_of(i) * SHARE + h * HALF, HALF)]
        return copy(src, dst, rp_s.at[u, i, h], rp_r.at[u, i, h], (base + i, d))

    for kind in (0, 1):
        for j in range(1, TEAM):
            team_weights(1, j, kind).start()

    def cot_copy(r):
        src = cot.at[pl.ds(pl.multiple_of(r * 2 * TILE, 2 * TILE), 2 * TILE)]
        return copy(src, window.at[s], cot_s.at[r], cot_r.at[s], (r, d))

    def to_first(body):
        def one(r):
            @pl.when(s != r)
            def _():
                body(r)

        repeat(0, TEAM, one)

    to_first(lambda r: cot_copy(r).start())

    def gather_copy(u, i, at, xs, cs, kind, dev):
        ref = piece(u, i, 2 * xs + cs, kind)
        return copy(ref, ref, gat_s.at[u, i, at], gat_r.at[u, i, at], dev)

    def gather_sends(u, i):
        return [
            gather_copy(u, i, 0, x, c, 0, dev_right),
            gather_copy(u, i, 1, x, c, 1, dev_right),
            gather_copy(u, i, 2, x, c, 0, dev_left),
            gather_copy(u, i, 3, x, c, 1, dev_left),
            gather_copy(u, i, 4, left, c, 0, dev_right),
            gather_copy(u, i, 5, right, c, 1, dev_left),
        ] + [
            gather_copy(u, i, 6 + 2 * n + kind, xs, c, kind, sib)
            for n, xs in enumerate((x, left, right, far))
            for kind in (0, 1)
        ]

    def gather_recvs(u, i):
        return [
            gather_copy(u, i, 0, left, c, 0, dev_left),
            gather_copy(u, i, 1, left, c, 1, dev_left),
            gather_copy(u, i, 2, right, c, 0, dev_right),
            gather_copy(u, i, 3, right, c, 1, dev_right),
            gather_copy(u, i, 4, far, c, 0, dev_left),
            gather_copy(u, i, 5, far, c, 1, dev_right),
        ] + [
            gather_copy(u, i, 6 + 2 * n + kind, xs, 1 - c, kind, sib)
            for n, xs in enumerate((x, left, right, far))
            for kind in (0, 1)
        ]

    def gather_open(u, i):
        out = gather_sends(u, i)
        for n in (0, 3, 1, 2, 6, 7):
            out[n].start()

    def gather_close(u, i):
        out, arr = gather_sends(u, i), gather_recvs(u, i)
        arr[0].wait_recv()
        out[4].start()
        out[8].start()
        arr[3].wait_recv()
        out[5].start()
        out[11].start()
        arr[1].wait_recv()
        out[9].start()
        arr[2].wait_recv()
        out[10].start()
        arr[4].wait_recv()
        out[12].start()
        arr[5].wait_recv()
        out[13].start()
        for n in range(6, 14):
            arr[n].wait_recv()

    def gather_next(u, j):
        for kind in (0, 1):
            team_weights_in(u, j, kind).wait_recv()
        gather_open(u, mate(j))

    def gates(u):
        flat = MICRO * TILE
        pre = jnp.zeros((flat, RANK), F32)
        squares = jnp.zeros((flat, 1), F32)
        for e in range(N_DP):
            part = stash[u, :, :, e * SHARD : (e + 1) * SHARD].reshape(flat, SHARD)
            wide = part.astype(F32)
            squares = squares + jnp.sum(wide * wide, axis=1, keepdims=True)
            q, off = e // PER_PART, (e % PER_PART) * SHARD
            pre = pre + lax.dot_general(
                part, w_a[u, own, q * RANK : (q + 1) * RANK, off : off + SHARD], NT, preferred_element_type=F32
            )
        inv = lax.rsqrt(squares * (1.0 / D) + norm_epsilon)
        pre = pre * inv
        sig = 1.0 / (1.0 + jnp.exp(-pre))
        hidden = pre * sig
        turn = sig * (1.0 + pre * (1.0 - sig)) * inv
        lean = pre * inv * (1.0 / D)
        for m in range(MICRO):
            for j in range(FOLD):
                here = m * FOLD + j
                rows = slice(m * TILE, (m + 1) * TILE)
                gates_own[u, here, 0] = spread(jnp.where(group == j, turn[rows], 0.0))
                gates_own[u, here, 1] = spread(jnp.where(group == j, lean[rows], 0.0))
                hid[u, here] = spread(jnp.where(group == j, hidden[rows], 0.0)).astype(BF16)

    def give_x(u):
        for j in range(1, TEAM):
            share_x(u, j).start()

        def keep_own(k):
            x_slot[u, own, k] = x_fold[u, mine + k]

        repeat(0, SHARE, keep_own)

    def give_gates(u):
        gates(u)
        for j in range(1, TEAM):
            share_gates(u, j).start()

        def keep_own(k):
            gates_slot[u, own, k] = gates_own[u, mine + k]

        repeat(0, SHARE, keep_own)

    def take(u):
        for j in range(1, TEAM):
            share_x_in(u, j).wait_recv()
            share_gates_in(u, j).wait_recv()

    gather_open(1, own)
    fold_stash(1)
    gather_close(1, own)
    give_gates(1)
    repeat(1, TEAM, lambda j: gather_next(1, j))
    give_x(1)

    @pl.when(first)
    def _():
        window[s] = cot[pl.ds(pl.multiple_of(s * 2 * TILE, 2 * TILE), 2 * TILE), :]

        def arrive(i):
            copy(
                cot.at[pl.ds(0, 2 * TILE)], window.at[lax.rem(s + i, N_SECTION)], cot_s.at[0],
                cot_r.at[lax.rem(s + i, N_SECTION)], sib,
            ).wait_recv()

        repeat(1, N_SECTION, arrive)

        def tile(q, at, m):
            column = (q * WIDE + at) // RANK
            start, place = column // 5 * 4, column % 5
            rows = slice(m * TILE, (m + 1) * TILE)
            value = None
            if place < 4:
                value = window[start + place, rows, :RANK].astype(F32)
            if place > 0:
                other = window[start + place - 1, rows, RANK:].astype(F32)
                value = other if value is None else value + other
            return value

        for m in range(2):
            def put(j, at, value):
                d_slot[1, 0, m * FOLD + j, :, at : at + RANK] = value

            refold(lambda q, at: tile(q, at, m), put)

    repeat(1, TEAM, lambda j: gather_close(1, mate(j)))
    for kind in (0, 1):
        for j in range(1, TEAM):
            team_weights(0, j, kind).start()
    gather_open(0, own)
    take(1)

    def lower_inputs():
        fold_stash(0)
        give_x(0)

    def lower_gates():
        gather_close(0, own)
        give_gates(0)

    def lower_open():
        repeat(1, TEAM, lambda j: gather_next(0, j))

    def lower_close():
        repeat(1, TEAM, lambda j: gather_close(0, mate(j)))

    pl.when(team >= INPUTS)(lower_inputs)
    pl.when(team >= GATES)(lower_gates)
    pl.when(team >= OPEN)(lower_open)

    @pl.when(team >= LATE)
    def _():
        lower_close()
        take(0)

    def chain_copy(u, k, dev):
        place = d_slot.at[1, 0, k] if u == 1 else d_slot.at[0, TEAM - 1, k]
        return copy(d_out.at[u, k], place, ch_s.at[u, k], ch_r.at[u, k], dev)

    def block(u, i, k, incoming):
        wide = jnp.dot(incoming, w_b[u, i], preferred_element_type=F32)
        picked = jnp.where(group == 0, wide[:, :RANK], 0.0)
        for q in range(1, FOLD):
            picked = jnp.where(group == q, wide[:, q * RANK : (q + 1) * RANK], picked)
        grad_hidden = spread(picked)
        small = (grad_hidden * gates_slot[u, i, k, 0]).astype(BF16)
        p_slot[u, i, k] = small
        grad_pre = small.astype(F32)
        shift = jnp.sum(grad_pre * gates_slot[u, i, k, 1], axis=1, keepdims=True)
        diag = diagonal(grad_pre, group).astype(BF16)
        back = jnp.dot(diag, w_a[u, i], preferred_element_type=F32)
        return (incoming.astype(F32) + back - x_slot[u, i, k].astype(F32) * shift).astype(BF16)

    def walk(u, k):
        order = list(range(TEAM)) if u == 1 else list(range(TEAM))[::-1]
        value = d_slot[u, order[0], k]
        for n, i in enumerate(order):
            value = block(u, i, k, value)
            if n < TEAM - 1:
                d_slot[u, order[n + 1], k] = value
        return value

    def upper(k):
        @pl.when(team > 0)
        def _():
            chain_copy(1, k, up).wait_recv()

        out = walk(1, k)

        @pl.when(last)
        def _():
            d_slot[0, TEAM - 1, k] = out

        @pl.when(team < TEAMS - 1)
        def _():
            d_out[1, k] = out
            chain_copy(1, k, down).start()

    def give_back(u, h):
        for j in range(1, TEAM):
            back_d(u, j, h).start()
            back_p(u, j, h).start()

    def lower(k):
        @pl.when(team < TEAMS - 1)
        def _():
            chain_copy(0, k, down).wait_recv()

        out = walk(0, k)

        @pl.when(team > 0)
        def _():
            d_out[0, k] = out
            chain_copy(0, k, up).start()

        @pl.when(first & (k == HALF - 1))
        def _():
            give_back(0, 0)

    def partial(u, kind, e):
        q = e // PER_PART
        col = pl.multiple_of((e % PER_PART) * SHARD, SHARD)
        rows = CHUNKS * TILE
        small = hid[u] if kind == 0 else p_in[u]
        right_side = d_in if kind == 0 else x_fold
        lhs = (small * mask[q][None]).reshape(rows, RANK)
        rhs = right_side[u, :, :, pl.ds(col, SHARD)].reshape(rows, SHARD)
        return lax.dot_general(lhs, rhs, TN, preferred_element_type=F32)

    def pair_copy(u, kind):
        return copy(pair_out.at[u, kind], pair_in.at[u, kind], pair_s.at[u, kind], pair_r.at[u, kind], sib)

    def ring_copy(u, kind, at, dev):
        return copy(ring_out.at[u, kind, at], ring_in.at[u, kind, at], ring_s.at[u, kind, at], ring_r.at[u, kind, at], dev)

    def gradients(u):
        def keep_own(k):
            d_in[u, mine + k] = d_slot[u, own, k]
            p_in[u, mine + k] = p_slot[u, own, k]

        repeat(0, SHARE, keep_own)
        for j in range(1, TEAM):
            for h in (0, 1):
                back_d_in(u, j, h).wait_recv()
                back_p_in(u, j, h).wait_recv()
        for kind in (0, 1):
            def theirs(i):
                pair_out[u, kind, i] = partial(u, kind, 2 * i + 1 - c).astype(BF16)

            repeat(0, N_X, theirs)
            pair_copy(u, kind).start()
        for kind in (0, 1):
            def ours(i):
                keep[kind, i] = partial(u, kind, 2 * i + c)

            repeat(0, N_X, ours)
        ways = ((dev_right, right, dev_left, left), (dev_left, left, dev_right, right))
        for kind in (0, 1):
            ahead, ahead_x, behind, behind_x = ways[kind]
            pair_copy(u, kind).wait_recv()
            keep[kind] = keep[kind] + pair_in[u, kind].astype(F32)
            ring_out[u, kind, 0] = keep[kind, far].astype(BF16)
            ring_copy(u, kind, 0, ahead).start()
            ring_out[u, kind, 1] = keep[kind, behind_x].astype(BF16)
            ring_copy(u, kind, 1, behind).start()
        for kind in (0, 1):
            ahead, ahead_x, behind, behind_x = ways[kind]
            ring_copy(u, kind, 0, behind).wait_recv()
            ring_out[u, kind, 2] = (keep[kind, ahead_x] + ring_in[u, kind, 0].astype(F32)).astype(BF16)
            ring_copy(u, kind, 2, ahead).start()
        squares = jnp.zeros((1, 1), F32)
        for kind in (0, 1):
            ahead, ahead_x, behind, behind_x = ways[kind]
            ring_copy(u, kind, 1, ahead).wait_recv()
            ring_copy(u, kind, 2, behind).wait_recv()
            grad = keep[kind, x] + ring_in[u, kind, 1].astype(F32) + ring_in[u, kind, 2].astype(F32)
            squares = squares + jnp.sum(jnp.sum(grad * grad, axis=0, keepdims=True), axis=1, keepdims=True)
            if kind == 0:
                grad_b[u] = grad
            else:
                grad_a[u] = grad.T
        norm_out[...] = norm_out[...] + jnp.broadcast_to(squares, (8, 128))

    norm_out[...] = jnp.zeros((8, 128), F32)

    lag = jnp.where(team < LATE, SHARE, jnp.minimum(SHARE, LAG * (TEAMS - 1 - team)))

    def tick(t):
        upper(t)

        @pl.when(t >= lag)
        def _():
            lower(t - lag)

    repeat(0, SHARE, tick)

    def back_upper():
        for h in (0, 1):
            give_back(1, h)

    pl.when(team < INPUTS)(lower_inputs)
    pl.when(team < GATES)(lower_gates)
    pl.when(team < OPEN)(lower_open)
    pl.when(team < LATE)(lower_close)
    pl.when(team < BACK)(back_upper)
    pl.when(team < EARLY)(lambda: gradients(1))
    pl.when(team < LATE)(lambda: take(0))
    repeat(SHARE - lag, SHARE, lower)
    pl.when(team >= BACK)(back_upper)
    pl.when(team > 0)(lambda: give_back(0, 0))
    give_back(0, 1)
    pl.when(team >= EARLY)(lambda: gradients(1))
    gradients(0)

    @pl.when(s > 0)
    def _():
        up_copy = copy(norm_out, norm_in.at[s], nrm_s, nrm_r.at[s], home)
        up_copy.start()
        copy(lane_out, tot_in, lan_s.at[0], tot_r, home).wait_recv()
        total[...] = tot_in[...]
        up_copy.wait_send()

    @pl.when(s == 0)
    def _():
        norm_in[0] = norm_out[...]
        repeat(1, N_SECTION, lambda i: copy(norm_out, norm_in.at[i], nrm_s, nrm_r.at[i], sib).wait_recv())
        lane_out[...] = jnp.sum(norm_in[...], axis=0)

        def share(i):
            return copy(lane_out, lane_in.at[i], lan_s.at[i], lan_r.at[i], (0, lax.rem(d + i, N_DP)))

        for i in range(1, N_DP):
            share(i).start()
        for i in range(1, N_DP):
            share(i).wait_recv()
        lane_in[0] = lane_out[...]
        value = jnp.sum(lane_in[...], axis=0)
        total[...] = value
        norm_out[...] = value
        repeat(1, N_SECTION, lambda i: copy(norm_out, tot_in, tot_s.at[i], tot_r, (i, d)).start())
        repeat(1, N_SECTION, lambda i: copy(norm_out, tot_in, tot_s.at[i], tot_r, (i, d)).wait_send())
        for i in range(1, N_DP):
            share(i).wait_send()

    to_first(lambda r: cot_copy(r).wait_send())
    for u in (0, 1):
        def sent(j):
            for one in gather_sends(u, mate(j)):
                one.wait_send()

        repeat(0, TEAM, sent)
        for kind in (0, 1):
            pair_copy(u, kind).wait_send()
            for at in range(3):
                ring_copy(u, kind, at, sib).wait_send()

        def given(j):
            for kind in (0, 1):
                team_weights(u, j, kind).wait_send()
            share_x(u, j).wait_send()
            share_gates(u, j).wait_send()
            for h in (0, 1):
                back_d(u, j, h).wait_send()
                back_p(u, j, h).wait_send()

        repeat(1, TEAM, given)

    @pl.when(team < TEAMS - 1)
    def _():
        repeat(0, SHARE, lambda k: chain_copy(1, k, down).wait_send())

    @pl.when(team > 0)
    def _():
        repeat(0, SHARE, lambda k: chain_copy(0, k, up).wait_send())


def chain(stash, cot, a_param, b_param):
    dma = pltpu.SemaphoreType.DMA
    vmem = pl.BlockSpec(memory_space=pltpu.VMEM)
    part = (2, 2, N_X, RANK, SHARD)
    own_rows = (2, CHUNKS, TILE)
    slot_rows = (2, TEAM, SHARE, TILE)
    return pl.pallas_call(
        chain_kernel,
        name="chain",
        out_shape=(
            jax.ShapeDtypeStruct((2, SHARD, RANK), F32),
            jax.ShapeDtypeStruct((2, RANK, SHARD), F32),
            jax.ShapeDtypeStruct((8, 128), F32),
        ),
        in_specs=[vmem] * 4,
        out_specs=(vmem,) * 3,
        scratch_shapes=[
            pltpu.VMEM((2, TEAM, WIDE, FOLD * RANK), BF16),
            pltpu.VMEM((2, TEAM, FOLD * RANK, WIDE), BF16),
            pltpu.VMEM(own_rows + (WIDE,), BF16),
            pltpu.VMEM((2, CHUNKS, 2, TILE, RANK), F32),
            pltpu.VMEM(own_rows + (RANK,), BF16),
            pltpu.VMEM(own_rows + (WIDE,), BF16),
            pltpu.VMEM(own_rows + (RANK,), BF16),
            pltpu.VMEM(slot_rows + (WIDE,), BF16),
            pltpu.VMEM((2, TEAM, SHARE, 2, TILE, RANK), F32),
            pltpu.VMEM(slot_rows + (WIDE,), BF16),
            pltpu.VMEM(slot_rows + (RANK,), BF16),
            pltpu.VMEM((2, SHARE, TILE, WIDE), BF16),
            pltpu.VMEM((N_SECTION, 2 * TILE, 2 * RANK), BF16),
            pltpu.VMEM((FOLD, TILE, RANK), BF16),
            pltpu.VMEM((2, N_X, RANK, SHARD), F32),
            pltpu.VMEM(part, BF16),
            pltpu.VMEM(part, BF16),
            pltpu.VMEM((2, 2, 3, RANK, SHARD), BF16),
            pltpu.VMEM((2, 2, 3, RANK, SHARD), BF16),
            pltpu.VMEM((8, 128), F32),
            pltpu.VMEM((N_SECTION, 8, 128), F32),
            pltpu.VMEM((8, 128), F32),
            pltpu.VMEM((N_DP, 8, 128), F32),
            pltpu.VMEM((8, 128), F32),
            dma((2, 2, TEAM)), dma((2, 2, TEAM)),
            dma((2, TEAM, 14)), dma((2, TEAM, 14)),
            dma((2, TEAM)), dma((2, TEAM)),
            dma((2, TEAM)), dma((2, TEAM)),
            dma((2, TEAM, 2)), dma((2, TEAM, 2)),
            dma((2, TEAM, 2)), dma((2, TEAM, 2)),
            dma((2, SHARE)), dma((2, SHARE)),
            dma((TEAM,)), dma((N_SECTION,)),
            dma((2, 2)), dma((2, 2)),
            dma((2, 2, 3)), dma((2, 2, 3)),
            dma, dma((N_SECTION,)),
            dma((N_DP,)), dma((N_DP,)),
            dma((N_SECTION,)), dma,
        ],
        compiler_params=pltpu.CompilerParams(collective_id=0, has_side_effects=True, vmem_limit_bytes=60 << 20),
    )(stash, cot, a_param, b_param)


def adam_update(param, moment, second, grad, clip_factor):
    scaled = clip_factor * grad
    moment_new = beta_one * moment + (1.0 - beta_one) * scaled
    second_new = beta_two * second + (1.0 - beta_two) * scaled * scaled
    param_new = param - learning_rate * moment_new / (jnp.sqrt(second_new) + adam_epsilon)
    return (param_new, moment_new, second_new)


def shards(stash, cotangent, a_param, a_moment, a_second, b_param, b_moment, b_second):
    position = lax.axis_index("section")
    flat = cotangent.reshape(MICRO * TILE, D // N_SECTION)
    cot = lax.dynamic_update_slice(
        jnp.zeros((MICRO * TILE, 2 * RANK), BF16), flat, (0, 32 * lax.rem(position, 4))
    )
    grad_a, grad_b, total = chain(stash[:, 0], cot, a_param[:, 0], b_param[:, 0])
    grad_norm = jnp.sqrt(total[0, 0])
    entries = 4 * N_SECTION * D * RANK
    clip_factor = jnp.minimum(1.0, 0.5 * math.sqrt(entries) / grad_norm)
    a_new, a_moment_new, a_second_new = adam_update(a_param, a_moment, a_second, grad_a[:, None], clip_factor)
    b_new, b_moment_new, b_second_new = adam_update(b_param, b_moment, b_second, grad_b[:, None], clip_factor)
    return (a_new, a_moment_new, a_second_new, b_new, b_moment_new, b_second_new, grad_norm)


def solution(mesh):
    return jax.shard_map(
        shards,
        mesh=mesh,
        in_specs=(
            P(None, "section", None, "dp", None),
            P(None, "dp", "section"),
            P(None, "section", "dp", None),
            P(None, "section", "dp", None),
            P(None, "section", "dp", None),
            P(None, "section", None, "dp"),
            P(None, "section", None, "dp"),
            P(None, "section", None, "dp"),
        ),
        out_specs=(
            P(None, "section", "dp", None),
            P(None, "section", "dp", None),
            P(None, "section", "dp", None),
            P(None, "section", None, "dp"),
            P(None, "section", None, "dp"),
            P(None, "section", None, "dp"),
            P(),
        ),
        check_vma=False,
    )
```

```python
import functools
import math

import jax
import jax.numpy as jnp
from jax import lax
from jax.experimental import pallas as pl
from jax.experimental.pallas import tpu as pltpu
from jax.sharding import PartitionSpec as P

beta_one = 0.9
beta_two = 0.95
learning_rate = 0.01
adam_epsilon = 1e-08
norm_epsilon = 1e-06

MESH = pl.DeviceIdType.MESH
F32 = jnp.float32
BF16 = jnp.bfloat16

N_SECTION = 32
N_Z = 8
N_X = 4
N_DP = 8
D = 5120
RANK = 128
MICRO = 8
TILE = 16
SHARD = D // N_DP
FOLD = 4
ROWS = TILE // FOLD
CHUNKS = MICRO * FOLD
WIDE = D // FOLD
PER_PART = WIDE // SHARD
TEAM = 4
TEAMS = N_SECTION // TEAM
SHARE = CHUNKS // TEAM
PARTS = 4
PART = SHARE // PARTS
WEIGHTS, INPUTS, GATES, OPEN, LATE = 0, 1, 2, 3, 7
BACK = 6
EARLY = 3
LAG = 5

NT = (((1,), (1,)), ((), ()))
TN = (((0,), (0,)), ((), ()))


def row_group():
    return lax.broadcasted_iota(jnp.int32, (TILE, RANK), 0) // ROWS


def spread(value):
    step = TILE // 2
    while step >= ROWS:
        value = value + pltpu.roll(value, step, 0)
        step //= 2
    return value


def diagonal(value, group):
    return jnp.concatenate([jnp.where(group == q, value, 0.0) for q in range(FOLD)], axis=1)


def chain_kernel(
    stash, cot, a_param, b_param,
    grad_a, grad_b, total,
    w_b, w_a, x_fold, gates_own, hid, d_in, p_in, x_slot, gates_slot, d_slot, p_slot, d_out, window, mask,
    keep, pair_out, pair_in, ring_out, ring_in, norm_out, norm_in, lane_out, lane_in, tot_in,
    zw_s, zw_r, gat_s, gat_r, dx_s, dx_r, dg_s, dg_r, rd_s, rd_r, rp_s, rp_r, ch_s, ch_r, cot_s, cot_r,
    pair_s, pair_r, ring_s, ring_r, nrm_s, nrm_r, lan_s, lan_r, tot_s, tot_r,
):
    s = lax.axis_index("section")
    d = lax.axis_index("dp")
    x = d // 2
    c = d % 2
    right = lax.rem(x + 1, N_X)
    left = lax.rem(x + N_X - 1, N_X)
    far = lax.rem(x + 2, N_X)
    sib = (s, 2 * x + 1 - c)
    dev_right = (s, 2 * right + c)
    dev_left = (s, 2 * left + c)
    team = s // TEAM
    own = s % TEAM
    odd = team % 2
    base = team * TEAM

    def slot_of(i):
        return i + odd * (TEAM - 1 - 2 * i)

    slot = slot_of(own)
    mine = slot * SHARE
    first = team == 0
    last = team == TEAMS - 1
    down = (jnp.minimum(base + TEAM + TEAM - 1 - own, N_SECTION - 1), d)
    up = (jnp.maximum(base - 1 - own, 0), d)
    home = (0, d)
    group = row_group()

    def mate(j):
        return lax.rem(own + j, TEAM)

    def copy(src, dst, ssem, rsem, dev):
        return pltpu.make_async_remote_copy(
            src_ref=src, dst_ref=dst, send_sem=ssem, recv_sem=rsem, device_id=dev, device_id_type=MESH
        )

    def repeat(low, high, body):
        def step(i, carry):
            body(i)
            return carry

        lax.fori_loop(low, high, step, 0)

    bar = pltpu.get_barrier_semaphore()

    def hello(dev):
        pl.semaphore_signal(bar, inc=1, device_id=dev, device_id_type=MESH)

    hello(sib)
    hello(dev_right)
    hello(dev_left)
    for j in range(1, TEAM):
        hello((base + mate(j), d))

    @pl.when(team > 0)
    def _():
        hello(up)

    @pl.when(team < TEAMS - 1)
    def _():
        hello(down)

    @pl.when(s > 0)
    def _():
        hello(home)

    @pl.when(first)
    def _():
        repeat(1, N_SECTION, lambda i: hello((lax.rem(s + i, N_SECTION), d)))

    @pl.when(s == 0)
    def _():
        repeat(1, N_DP, lambda i: hello((0, lax.rem(d + i, N_DP))))

    def b_slice(u, i, e):
        row = pl.multiple_of((e % PER_PART) * SHARD, SHARD)
        col = pl.multiple_of((e // PER_PART) * RANK, RANK)
        return w_b.at[u, i, pl.ds(row, SHARD), pl.ds(col, RANK)]

    def a_slice(u, i, e):
        row = pl.multiple_of((e // PER_PART) * RANK, RANK)
        col = pl.multiple_of((e % PER_PART) * SHARD, SHARD)
        return w_a.at[u, i, pl.ds(row, RANK), pl.ds(col, SHARD)]

    def piece(u, i, e, kind):
        return b_slice(u, i, e) if kind == 0 else a_slice(u, i, e)

    def own_weights(u):
        b_slice(u, own, d)[...] = b_param[u].T.astype(BF16)
        a_slice(u, own, d)[...] = a_param[u].T.astype(BF16)

    def refold(get, put):
        for at in range(0, WIDE, RANK):
            parts = [get(q, at) for q in range(FOLD)]
            outs = [None] * FOLD
            for q in range(FOLD):
                for j in range(FOLD):
                    turn = (ROWS * (q - j)) % TILE
                    moved = parts[q] if turn == 0 else pltpu.roll(parts[q], turn, 0)
                    outs[j] = moved if q == 0 else jnp.where(group == q, moved, outs[j])
            for j in range(FOLD):
                put(j, at, outs[j].astype(BF16))

    def fold_stash(u):
        def micro(m):
            def put(j, at, value):
                x_fold[u, m * FOLD + j, :, at : at + RANK] = value

            refold(lambda q, at: stash[u, m, :, q * WIDE + at : q * WIDE + at + RANK].astype(F32), put)

        repeat(0, MICRO, micro)

    own_weights(1)
    for q in range(FOLD):
        mask[q] = jnp.where(group == q, 1.0, 0.0).astype(BF16)

    pl.semaphore_wait(
        bar,
        6
        + (team > 0).astype(jnp.int32)
        + (team < TEAMS - 1).astype(jnp.int32)
        + jnp.where(first, TEAM - 1, TEAM)
        + jnp.where(s == 0, N_SECTION + N_DP - 2, 0),
    )

    def team_weights(u, j, kind):
        i = mate(j)
        ref = piece(u, own, d, kind)
        return copy(ref, ref, zw_s.at[u, kind, i], zw_r.at[u, kind, own], (base + i, d))

    def team_weights_in(u, j, kind):
        i = mate(j)
        ref = piece(u, i, d, kind)
        return copy(ref, ref, zw_s.at[u, kind, i], zw_r.at[u, kind, i], (base + i, d))

    def share_x(u, j):
        i = mate(j)
        src = x_fold.at[u, pl.ds(slot_of(i) * SHARE, SHARE)]
        return copy(src, x_slot.at[u, own], dx_s.at[u, i], dx_r.at[u, own], (base + i, d))

    def share_x_in(u, j):
        i = mate(j)
        src = x_fold.at[u, pl.ds(mine, SHARE)]
        return copy(src, x_slot.at[u, i], dx_s.at[u, i], dx_r.at[u, i], (base + i, d))

    def share_gates(u, j):
        i = mate(j)
        src = gates_own.at[u, pl.ds(slot_of(i) * SHARE, SHARE)]
        return copy(src, gates_slot.at[u, own], dg_s.at[u, i], dg_r.at[u, own], (base + i, d))

    def share_gates_in(u, j):
        i = mate(j)
        src = gates_own.at[u, pl.ds(mine, SHARE)]
        return copy(src, gates_slot.at[u, i], dg_s.at[u, i], dg_r.at[u, i], (base + i, d))

    def back_d(u, j, h):
        i = mate(j)
        src = d_slot.at[u, i, pl.ds(h * PART, PART)]
        dst = d_in.at[u, pl.ds(mine + h * PART, PART)]
        return copy(src, dst, rd_s.at[u, i, h], rd_r.at[u, own, h], (base + i, d))

    def back_d_in(u, j, h):
        i = mate(j)
        src = d_slot.at[u, i, pl.ds(h * PART, PART)]
        dst = d_in.at[u, pl.ds(slot_of(i) * SHARE + h * PART, PART)]
        return copy(src, dst, rd_s.at[u, i, h], rd_r.at[u, i, h], (base + i, d))

    def back_p(u, j, h):
        i = mate(j)
        src = p_slot.at[u, i, pl.ds(h * PART, PART)]
        dst = p_in.at[u, pl.ds(mine + h * PART, PART)]
        return copy(src, dst, rp_s.at[u, i, h], rp_r.at[u, own, h], (base + i, d))

    def back_p_in(u, j, h):
        i = mate(j)
        src = p_slot.at[u, i, pl.ds(h * PART, PART)]
        dst = p_in.at[u, pl.ds(slot_of(i) * SHARE + h * PART, PART)]
        return copy(src, dst, rp_s.at[u, i, h], rp_r.at[u, i, h], (base + i, d))

    for kind in (0, 1):
        for j in range(1, TEAM):
            team_weights(1, j, kind).start()

    def cot_copy(r):
        src = cot.at[pl.ds(pl.multiple_of(r * 2 * TILE, 2 * TILE), 2 * TILE)]
        return copy(src, window.at[s], cot_s.at[r], cot_r.at[s], (r, d))

    def to_first(body):
        def one(r):
            @pl.when(s != r)
            def _():
                body(r)

        repeat(0, TEAM, one)

    to_first(lambda r: cot_copy(r).start())

    def gather_copy(u, i, at, xs, cs, kind, dev):
        ref = piece(u, i, 2 * xs + cs, kind)
        return copy(ref, ref, gat_s.at[u, i, at], gat_r.at[u, i, at], dev)

    def gather_sends(u, i):
        return [
            gather_copy(u, i, 0, x, c, 0, dev_right),
            gather_copy(u, i, 1, x, c, 1, dev_right),
            gather_copy(u, i, 2, x, c, 0, dev_left),
            gather_copy(u, i, 3, x, c, 1, dev_left),
            gather_copy(u, i, 4, left, c, 0, dev_right),
            gather_copy(u, i, 5, right, c, 1, dev_left),
        ] + [
            gather_copy(u, i, 6 + 2 * n + kind, xs, c, kind, sib)
            for n, xs in enumerate((x, left, right, far))
            for kind in (0, 1)
        ]

    def gather_recvs(u, i):
        return [
            gather_copy(u, i, 0, left, c, 0, dev_left),
            gather_copy(u, i, 1, left, c, 1, dev_left),
            gather_copy(u, i, 2, right, c, 0, dev_right),
            gather_copy(u, i, 3, right, c, 1, dev_right),
            gather_copy(u, i, 4, far, c, 0, dev_left),
            gather_copy(u, i, 5, far, c, 1, dev_right),
        ] + [
            gather_copy(u, i, 6 + 2 * n + kind, xs, 1 - c, kind, sib)
            for n, xs in enumerate((x, left, right, far))
            for kind in (0, 1)
        ]

    def gather_open(u, i):
        out = gather_sends(u, i)
        for n in (0, 3, 1, 2, 6, 7):
            out[n].start()

    def gather_close(u, i):
        out, arr = gather_sends(u, i), gather_recvs(u, i)
        arr[0].wait_recv()
        out[4].start()
        out[8].start()
        arr[3].wait_recv()
        out[5].start()
        out[11].start()
        arr[1].wait_recv()
        out[9].start()
        arr[2].wait_recv()
        out[10].start()
        arr[4].wait_recv()
        out[12].start()
        arr[5].wait_recv()
        out[13].start()
        for n in range(6, 14):
            arr[n].wait_recv()

    def gather_next(u, j):
        for kind in (0, 1):
            team_weights_in(u, j, kind).wait_recv()
        gather_open(u, mate(j))

    def gates(u):
        flat = MICRO * TILE
        pre = jnp.zeros((flat, RANK), F32)
        squares = jnp.zeros((flat, 1), F32)
        for e in range(N_DP):
            part = stash[u, :, :, e * SHARD : (e + 1) * SHARD].reshape(flat, SHARD)
            wide = part.astype(F32)
            squares = squares + jnp.sum(wide * wide, axis=1, keepdims=True)
            q, off = e // PER_PART, (e % PER_PART) * SHARD
            pre = pre + lax.dot_general(
                part, w_a[u, own, q * RANK : (q + 1) * RANK, off : off + SHARD], NT, preferred_element_type=F32
            )
        inv = lax.rsqrt(squares * (1.0 / D) + norm_epsilon)
        pre = pre * inv
        sig = 1.0 / (1.0 + jnp.exp(-pre))
        hidden = pre * sig
        turn = sig * (1.0 + pre * (1.0 - sig)) * inv
        lean = pre * inv * (1.0 / D)
        for m in range(MICRO):
            for j in range(FOLD):
                here = m * FOLD + j
                rows = slice(m * TILE, (m + 1) * TILE)
                gates_own[u, here, 0] = spread(jnp.where(group == j, turn[rows], 0.0))
                gates_own[u, here, 1] = spread(jnp.where(group == j, lean[rows], 0.0))
                hid[u, here] = spread(jnp.where(group == j, hidden[rows], 0.0)).astype(BF16)

    def give_x(u):
        for j in range(1, TEAM):
            share_x(u, j).start()

        def keep_own(k):
            x_slot[u, own, k] = x_fold[u, mine + k]

        repeat(0, SHARE, keep_own)

    def give_gates(u):
        gates(u)
        for j in range(1, TEAM):
            share_gates(u, j).start()

        def keep_own(k):
            gates_slot[u, own, k] = gates_own[u, mine + k]

        repeat(0, SHARE, keep_own)

    def take_x(u):
        for j in range(1, TEAM):
            share_x_in(u, j).wait_recv()

    def take_gates(u):
        for j in range(1, TEAM):
            share_gates_in(u, j).wait_recv()

    gather_open(1, own)
    own_weights(0)
    fold_stash(1)
    give_x(1)
    gather_close(1, own)
    give_gates(1)
    repeat(1, TEAM, lambda j: gather_next(1, j))
    fold_stash(0)

    @pl.when(first)
    def _():
        window[s] = cot[pl.ds(pl.multiple_of(s * 2 * TILE, 2 * TILE), 2 * TILE), :]

        def arrive(i):
            copy(
                cot.at[pl.ds(0, 2 * TILE)], window.at[lax.rem(s + i, N_SECTION)], cot_s.at[0],
                cot_r.at[lax.rem(s + i, N_SECTION)], sib,
            ).wait_recv()

        repeat(1, N_SECTION, arrive)

        def tile(q, at, m):
            column = (q * WIDE + at) // RANK
            start, place = column // 5 * 4, column % 5
            rows = slice(m * TILE, (m + 1) * TILE)
            value = None
            if place < 4:
                value = window[start + place, rows, :RANK].astype(F32)
            if place > 0:
                other = window[start + place - 1, rows, RANK:].astype(F32)
                value = other if value is None else value + other
            return value

        for m in range(2):
            def put(j, at, value):
                d_slot[1, 0, m * FOLD + j, :, at : at + RANK] = value

            refold(lambda q, at: tile(q, at, m), put)

    def lower_weights():
        for kind in (0, 1):
            for j in range(1, TEAM):
                team_weights(0, j, kind).start()

    def lower_inputs():
        give_x(0)

    take_x(1)
    pl.when(team >= WEIGHTS)(lower_weights)
    pl.when(team >= INPUTS)(lower_inputs)
    repeat(1, TEAM, lambda j: gather_close(1, mate(j)))
    gather_open(0, own)
    take_gates(1)

    def lower_gates():
        gather_close(0, own)
        give_gates(0)

    def lower_open():
        repeat(1, TEAM, lambda j: gather_next(0, j))

    def lower_close():
        repeat(1, TEAM, lambda j: gather_close(0, mate(j)))
        take_x(0)
        take_gates(0)

    pl.when(team >= GATES)(lower_gates)
    pl.when(team >= OPEN)(lower_open)

    pl.when(team >= LATE)(lower_close)

    def chain_copy(u, k, dev):
        place = d_slot.at[1, 0, k] if u == 1 else d_slot.at[0, TEAM - 1, k]
        return copy(d_out.at[u, k], place, ch_s.at[u, k], ch_r.at[u, k], dev)

    def block(u, i, k, incoming):
        wide = jnp.dot(incoming, w_b[u, i], preferred_element_type=F32)
        picked = jnp.where(group == 0, wide[:, :RANK], 0.0)
        for q in range(1, FOLD):
            picked = jnp.where(group == q, wide[:, q * RANK : (q + 1) * RANK], picked)
        grad_hidden = spread(picked)
        small = (grad_hidden * gates_slot[u, i, k, 0]).astype(BF16)
        p_slot[u, i, k] = small
        grad_pre = small.astype(F32)
        shift = jnp.sum(grad_pre * gates_slot[u, i, k, 1], axis=1, keepdims=True)
        diag = diagonal(grad_pre, group).astype(BF16)
        back = jnp.dot(diag, w_a[u, i], preferred_element_type=F32)
        return (incoming.astype(F32) + back - x_slot[u, i, k].astype(F32) * shift).astype(BF16)

    def walk(u, k):
        order = list(range(TEAM)) if u == 1 else list(range(TEAM))[::-1]
        value = d_slot[u, order[0], k]
        for n, i in enumerate(order):
            value = block(u, i, k, value)
            if n < TEAM - 1:
                d_slot[u, order[n + 1], k] = value
        return value

    def upper(k):
        @pl.when(team > 0)
        def _():
            chain_copy(1, k, up).wait_recv()

        out = walk(1, k)

        @pl.when(last)
        def _():
            d_slot[0, TEAM - 1, k] = out

        @pl.when(team < TEAMS - 1)
        def _():
            d_out[1, k] = out
            chain_copy(1, k, down).start()

    def give_back(u, h):
        for j in range(1, TEAM):
            back_d(u, j, h).start()
            back_p(u, j, h).start()

    def lower(k):
        @pl.when(team < TEAMS - 1)
        def _():
            chain_copy(0, k, down).wait_recv()

        out = walk(0, k)

        @pl.when(team > 0)
        def _():
            d_out[0, k] = out
            chain_copy(0, k, up).start()

        @pl.when(first & (k % PART == PART - 1) & (k < SHARE - 1))
        def _():
            give_back(0, k // PART)

    def partial(u, kind, h):
        rows = CHUNKS * TILE
        small = hid[u] if kind == 0 else p_in[u]
        right_side = d_in if kind == 0 else x_fold
        lhs = jnp.concatenate([small * mask[q][None] for q in range(FOLD)], axis=2).reshape(rows, FOLD * RANK)
        col = pl.multiple_of(h * SHARD, SHARD)
        rhs = right_side[u, :, :, pl.ds(col, SHARD)].reshape(rows, SHARD)
        return lax.dot_general(lhs, rhs, TN, preferred_element_type=F32).reshape(N_X, RANK, SHARD)

    def pair_copy(u, kind):
        return copy(pair_out.at[u, kind], pair_in.at[u, kind], pair_s.at[u, kind], pair_r.at[u, kind], sib)

    def ring_copy(u, kind, at, dev):
        return copy(ring_out.at[u, kind, at], ring_in.at[u, kind, at], ring_s.at[u, kind, at], ring_r.at[u, kind, at], dev)

    def gradients(u):
        def keep_own(k):
            d_in[u, mine + k] = d_slot[u, own, k]
            p_in[u, mine + k] = p_slot[u, own, k]

        repeat(0, SHARE, keep_own)
        for j in range(1, TEAM):
            for h in range(PARTS):
                back_d_in(u, j, h).wait_recv()
                back_p_in(u, j, h).wait_recv()
        for kind in (0, 1):
            pair_out[u, kind] = partial(u, kind, 1 - c).astype(BF16)
            pair_copy(u, kind).start()
        for kind in (0, 1):
            keep[kind] = partial(u, kind, c)
        ways = ((dev_right, right, dev_left, left), (dev_left, left, dev_right, right))
        for kind in (0, 1):
            ahead, ahead_x, behind, behind_x = ways[kind]
            pair_copy(u, kind).wait_recv()
            keep[kind] = keep[kind] + pair_in[u, kind].astype(F32)
            ring_out[u, kind, 0] = keep[kind, far].astype(BF16)
            ring_copy(u, kind, 0, ahead).start()
            ring_out[u, kind, 1] = keep[kind, behind_x].astype(BF16)
            ring_copy(u, kind, 1, behind).start()
        for kind in (0, 1):
            ahead, ahead_x, behind, behind_x = ways[kind]
            ring_copy(u, kind, 0, behind).wait_recv()
            ring_out[u, kind, 2] = (keep[kind, ahead_x] + ring_in[u, kind, 0].astype(F32)).astype(BF16)
            ring_copy(u, kind, 2, ahead).start()
        squares = jnp.zeros((1, 1), F32)
        for kind in (0, 1):
            ahead, ahead_x, behind, behind_x = ways[kind]
            ring_copy(u, kind, 1, ahead).wait_recv()
            ring_copy(u, kind, 2, behind).wait_recv()
            grad = keep[kind, x] + ring_in[u, kind, 1].astype(F32) + ring_in[u, kind, 2].astype(F32)
            squares = squares + jnp.sum(jnp.sum(grad * grad, axis=0, keepdims=True), axis=1, keepdims=True)
            if kind == 0:
                grad_b[u] = grad
            else:
                grad_a[u] = grad.T
        norm_out[...] = norm_out[...] + jnp.broadcast_to(squares, (8, 128))

    norm_out[...] = jnp.zeros((8, 128), F32)

    lag = jnp.where(team < LATE, SHARE, jnp.minimum(SHARE, LAG * (TEAMS - 1 - team)))

    def tick(t):
        upper(t)

        @pl.when(t >= lag)
        def _():
            lower(t - lag)

    repeat(0, SHARE, tick)

    def back_upper():
        repeat(0, PARTS, lambda h: give_back(1, h))

    pl.when(team < WEIGHTS)(lower_weights)
    pl.when(team < INPUTS)(lower_inputs)
    pl.when(team < GATES)(lower_gates)
    pl.when(team < OPEN)(lower_open)
    pl.when(team < LATE)(lower_close)
    pl.when(team < BACK)(back_upper)
    pl.when(team < EARLY)(lambda: gradients(1))
    repeat(SHARE - lag, SHARE, lower)
    pl.when(team >= BACK)(back_upper)
    pl.when(team > 0)(lambda: repeat(0, PARTS - 1, lambda h: give_back(0, h)))
    give_back(0, PARTS - 1)
    pl.when(team >= EARLY)(lambda: gradients(1))
    gradients(0)

    @pl.when(s > 0)
    def _():
        up_copy = copy(norm_out, norm_in.at[s], nrm_s, nrm_r.at[s], home)
        up_copy.start()
        copy(lane_out, tot_in, lan_s.at[0], tot_r, home).wait_recv()
        total[...] = tot_in[...]
        up_copy.wait_send()

    @pl.when(s == 0)
    def _():
        norm_in[0] = norm_out[...]
        repeat(1, N_SECTION, lambda i: copy(norm_out, norm_in.at[i], nrm_s, nrm_r.at[i], sib).wait_recv())
        lane_out[...] = jnp.sum(norm_in[...], axis=0)

        def share(i):
            return copy(lane_out, lane_in.at[i], lan_s.at[i], lan_r.at[i], (0, lax.rem(d + i, N_DP)))

        for i in range(1, N_DP):
            share(i).start()
        for i in range(1, N_DP):
            share(i).wait_recv()
        lane_in[0] = lane_out[...]
        value = jnp.sum(lane_in[...], axis=0)
        total[...] = value
        norm_out[...] = value
        repeat(1, N_SECTION, lambda i: copy(norm_out, tot_in, tot_s.at[i], tot_r, (i, d)).start())
        repeat(1, N_SECTION, lambda i: copy(norm_out, tot_in, tot_s.at[i], tot_r, (i, d)).wait_send())
        for i in range(1, N_DP):
            share(i).wait_send()

    to_first(lambda r: cot_copy(r).wait_send())
    for u in (0, 1):
        def sent(j):
            for one in gather_sends(u, mate(j)):
                one.wait_send()

        repeat(0, TEAM, sent)
        for kind in (0, 1):
            pair_copy(u, kind).wait_send()
            for at in range(3):
                ring_copy(u, kind, at, sib).wait_send()

        def given(j):
            for kind in (0, 1):
                team_weights(u, j, kind).wait_send()
            share_x(u, j).wait_send()
            share_gates(u, j).wait_send()
            for h in range(PARTS):
                back_d(u, j, h).wait_send()
                back_p(u, j, h).wait_send()

        repeat(1, TEAM, given)

    @pl.when(team < TEAMS - 1)
    def _():
        repeat(0, SHARE, lambda k: chain_copy(1, k, down).wait_send())

    @pl.when(team > 0)
    def _():
        repeat(0, SHARE, lambda k: chain_copy(0, k, up).wait_send())


def chain(stash, cot, a_param, b_param):
    dma = pltpu.SemaphoreType.DMA
    vmem = pl.BlockSpec(memory_space=pltpu.VMEM)
    part = (2, 2, N_X, RANK, SHARD)
    own_rows = (2, CHUNKS, TILE)
    slot_rows = (2, TEAM, SHARE, TILE)
    return pl.pallas_call(
        chain_kernel,
        name="chain",
        out_shape=(
            jax.ShapeDtypeStruct((2, SHARD, RANK), F32),
            jax.ShapeDtypeStruct((2, RANK, SHARD), F32),
            jax.ShapeDtypeStruct((8, 128), F32),
        ),
        in_specs=[vmem] * 4,
        out_specs=(vmem,) * 3,
        scratch_shapes=[
            pltpu.VMEM((2, TEAM, WIDE, FOLD * RANK), BF16),
            pltpu.VMEM((2, TEAM, FOLD * RANK, WIDE), BF16),
            pltpu.VMEM(own_rows + (WIDE,), BF16),
            pltpu.VMEM((2, CHUNKS, 2, TILE, RANK), F32),
            pltpu.VMEM(own_rows + (RANK,), BF16),
            pltpu.VMEM(own_rows + (WIDE,), BF16),
            pltpu.VMEM(own_rows + (RANK,), BF16),
            pltpu.VMEM(slot_rows + (WIDE,), BF16),
            pltpu.VMEM((2, TEAM, SHARE, 2, TILE, RANK), F32),
            pltpu.VMEM(slot_rows + (WIDE,), BF16),
            pltpu.VMEM(slot_rows + (RANK,), BF16),
            pltpu.VMEM((2, SHARE, TILE, WIDE), BF16),
            pltpu.VMEM((N_SECTION, 2 * TILE, 2 * RANK), BF16),
            pltpu.VMEM((FOLD, TILE, RANK), BF16),
            pltpu.VMEM((2, N_X, RANK, SHARD), F32),
            pltpu.VMEM(part, BF16),
            pltpu.VMEM(part, BF16),
            pltpu.VMEM((2, 2, 3, RANK, SHARD), BF16),
            pltpu.VMEM((2, 2, 3, RANK, SHARD), BF16),
            pltpu.VMEM((8, 128), F32),
            pltpu.VMEM((N_SECTION, 8, 128), F32),
            pltpu.VMEM((8, 128), F32),
            pltpu.VMEM((N_DP, 8, 128), F32),
            pltpu.VMEM((8, 128), F32),
            dma((2, 2, TEAM)), dma((2, 2, TEAM)),
            dma((2, TEAM, 14)), dma((2, TEAM, 14)),
            dma((2, TEAM)), dma((2, TEAM)),
            dma((2, TEAM)), dma((2, TEAM)),
            dma((2, TEAM, PARTS)), dma((2, TEAM, PARTS)),
            dma((2, TEAM, PARTS)), dma((2, TEAM, PARTS)),
            dma((2, SHARE)), dma((2, SHARE)),
            dma((TEAM,)), dma((N_SECTION,)),
            dma((2, 2)), dma((2, 2)),
            dma((2, 2, 3)), dma((2, 2, 3)),
            dma, dma((N_SECTION,)),
            dma((N_DP,)), dma((N_DP,)),
            dma((N_SECTION,)), dma,
        ],
        compiler_params=pltpu.CompilerParams(collective_id=0, has_side_effects=True, vmem_limit_bytes=60 << 20),
    )(stash, cot, a_param, b_param)


def adam_update(param, moment, second, grad, clip_factor):
    scaled = clip_factor * grad
    moment_new = beta_one * moment + (1.0 - beta_one) * scaled
    second_new = beta_two * second + (1.0 - beta_two) * scaled * scaled
    param_new = param - learning_rate * moment_new / (jnp.sqrt(second_new) + adam_epsilon)
    return (param_new, moment_new, second_new)


def shards(stash, cotangent, a_param, a_moment, a_second, b_param, b_moment, b_second):
    position = lax.axis_index("section")
    flat = cotangent.reshape(MICRO * TILE, D // N_SECTION)
    cot = lax.dynamic_update_slice(
        jnp.zeros((MICRO * TILE, 2 * RANK), BF16), flat, (0, 32 * lax.rem(position, 4))
    )
    grad_a, grad_b, total = chain(stash[:, 0], cot, a_param[:, 0], b_param[:, 0])
    grad_norm = jnp.sqrt(total[0, 0])
    entries = 4 * N_SECTION * D * RANK
    clip_factor = jnp.minimum(1.0, 0.5 * math.sqrt(entries) / grad_norm)
    a_new, a_moment_new, a_second_new = adam_update(a_param, a_moment, a_second, grad_a[:, None], clip_factor)
    b_new, b_moment_new, b_second_new = adam_update(b_param, b_moment, b_second, grad_b[:, None], clip_factor)
    return (a_new, a_moment_new, a_second_new, b_new, b_moment_new, b_second_new, grad_norm)


def solution(mesh):
    return jax.shard_map(
        shards,
        mesh=mesh,
        in_specs=(
            P(None, "section", None, "dp", None),
            P(None, "dp", "section"),
            P(None, "section", "dp", None),
            P(None, "section", "dp", None),
            P(None, "section", "dp", None),
            P(None, "section", None, "dp"),
            P(None, "section", None, "dp"),
            P(None, "section", None, "dp"),
        ),
        out_specs=(
            P(None, "section", "dp", None),
            P(None, "section", "dp", None),
            P(None, "section", "dp", None),
            P(None, "section", None, "dp"),
            P(None, "section", None, "dp"),
            P(None, "section", None, "dp"),
            P(),
        ),
        check_vma=False,
    )
```

```python
import functools
import math

import jax
import jax.numpy as jnp
from jax import lax
from jax.experimental import pallas as pl
from jax.experimental.pallas import tpu as pltpu
from jax.sharding import PartitionSpec as P

beta_one = 0.9
beta_two = 0.95
learning_rate = 0.01
adam_epsilon = 1e-08
norm_epsilon = 1e-06

MESH = pl.DeviceIdType.MESH
F32 = jnp.float32
BF16 = jnp.bfloat16

N_SECTION = 32
N_Z = 8
N_X = 4
N_DP = 8
D = 5120
RANK = 128
MICRO = 8
TILE = 16
SHARD = D // N_DP
FOLD = 4
ROWS = TILE // FOLD
CHUNKS = MICRO * FOLD
WIDE = D // FOLD
PER_PART = WIDE // SHARD
TEAM = 4
TEAMS = N_SECTION // TEAM
SHARE = CHUNKS // TEAM
PARTS = 4
PART = SHARE // PARTS
WEIGHTS, INPUTS, GATES, OPEN, LATE = 0, 1, 2, 3, 7
BACK = 6
EARLY = 3
LAG = 5

NT = (((1,), (1,)), ((), ()))
TN = (((0,), (0,)), ((), ()))


def row_group():
    return lax.broadcasted_iota(jnp.int32, (TILE, RANK), 0) // ROWS


def spread(value):
    step = TILE // 2
    while step >= ROWS:
        value = value + pltpu.roll(value, step, 0)
        step //= 2
    return value


def diagonal(value, group):
    return jnp.concatenate([jnp.where(group == q, value, 0.0) for q in range(FOLD)], axis=1)


def chain_kernel(
    stash, cot, a_param, b_param,
    grad_a, grad_b, total,
    w_b, w_a, x_fold, gates_own, hid, d_in, p_in, x_slot, gates_slot, d_slot, p_slot, d_out, window, mask,
    keep, pair_out, pair_in, ring_out, ring_in, norm_out, norm_in, lane_out, lane_in, tot_in,
    zw_s, zw_r, gat_s, gat_r, dx_s, dx_r, dg_s, dg_r, rd_s, rd_r, rp_s, rp_r, ch_s, ch_r, cot_s, cot_r,
    pair_s, pair_r, ring_s, ring_r, nrm_s, nrm_r, lan_s, lan_r, tot_s, tot_r,
):
    s = lax.axis_index("section")
    d = lax.axis_index("dp")
    x = d // 2
    c = d % 2
    right = lax.rem(x + 1, N_X)
    left = lax.rem(x + N_X - 1, N_X)
    far = lax.rem(x + 2, N_X)
    sib = (s, 2 * x + 1 - c)
    dev_right = (s, 2 * right + c)
    dev_left = (s, 2 * left + c)
    team = s // TEAM
    own = s % TEAM
    odd = team % 2
    base = team * TEAM

    def slot_of(i):
        return i + odd * (TEAM - 1 - 2 * i)

    slot = slot_of(own)
    mine = slot * SHARE
    first = team == 0
    last = team == TEAMS - 1
    down = (jnp.minimum(base + TEAM + TEAM - 1 - own, N_SECTION - 1), d)
    up = (jnp.maximum(base - 1 - own, 0), d)
    home = (0, d)
    group = row_group()

    def mate(j):
        return lax.rem(own + j, TEAM)

    def copy(src, dst, ssem, rsem, dev):
        return pltpu.make_async_remote_copy(
            src_ref=src, dst_ref=dst, send_sem=ssem, recv_sem=rsem, device_id=dev, device_id_type=MESH
        )

    def repeat(low, high, body):
        def step(i, carry):
            body(i)
            return carry

        lax.fori_loop(low, high, step, 0)

    bar = pltpu.get_barrier_semaphore()

    def hello(dev):
        pl.semaphore_signal(bar, inc=1, device_id=dev, device_id_type=MESH)

    hello(sib)
    hello(dev_right)
    hello(dev_left)
    for j in range(1, TEAM):
        hello((base + mate(j), d))

    @pl.when(team > 0)
    def _():
        hello(up)

    @pl.when(team < TEAMS - 1)
    def _():
        hello(down)

    @pl.when(s > 0)
    def _():
        hello(home)

    @pl.when(first)
    def _():
        repeat(1, N_SECTION, lambda i: hello((lax.rem(s + i, N_SECTION), d)))

    @pl.when(s == 0)
    def _():
        repeat(1, N_DP, lambda i: hello((0, lax.rem(d + i, N_DP))))

    def b_slice(u, i, e):
        row = pl.multiple_of((e % PER_PART) * SHARD, SHARD)
        col = pl.multiple_of((e // PER_PART) * RANK, RANK)
        return w_b.at[u, i, pl.ds(row, SHARD), pl.ds(col, RANK)]

    def a_slice(u, i, e):
        row = pl.multiple_of((e // PER_PART) * RANK, RANK)
        col = pl.multiple_of((e % PER_PART) * SHARD, SHARD)
        return w_a.at[u, i, pl.ds(row, RANK), pl.ds(col, SHARD)]

    def piece(u, i, e, kind):
        return b_slice(u, i, e) if kind == 0 else a_slice(u, i, e)

    def own_weights(u):
        b_slice(u, own, d)[...] = b_param[u].T.astype(BF16)
        a_slice(u, own, d)[...] = a_param[u].T.astype(BF16)

    def refold(get, put):
        for at in range(0, WIDE, RANK):
            parts = [get(q, at) for q in range(FOLD)]
            outs = [None] * FOLD
            for q in range(FOLD):
                for j in range(FOLD):
                    turn = (ROWS * (q - j)) % TILE
                    moved = parts[q] if turn == 0 else pltpu.roll(parts[q], turn, 0)
                    outs[j] = moved if q == 0 else jnp.where(group == q, moved, outs[j])
            for j in range(FOLD):
                put(j, at, outs[j].astype(BF16))

    def fold_stash(u):
        def micro(m):
            def put(j, at, value):
                x_fold[u, m * FOLD + j, :, at : at + RANK] = value

            refold(lambda q, at: stash[u, m, :, q * WIDE + at : q * WIDE + at + RANK].astype(F32), put)

        repeat(0, MICRO, micro)

    own_weights(1)
    for q in range(FOLD):
        mask[q] = jnp.where(group == q, 1.0, 0.0).astype(BF16)

    pl.semaphore_wait(
        bar,
        6
        + (team > 0).astype(jnp.int32)
        + (team < TEAMS - 1).astype(jnp.int32)
        + jnp.where(first, TEAM - 1, TEAM)
        + jnp.where(s == 0, N_SECTION + N_DP - 2, 0),
    )

    def team_weights(u, j, kind):
        i = mate(j)
        ref = piece(u, own, d, kind)
        return copy(ref, ref, zw_s.at[u, kind, i], zw_r.at[u, kind, own], (base + i, d))

    def team_weights_in(u, j, kind):
        i = mate(j)
        ref = piece(u, i, d, kind)
        return copy(ref, ref, zw_s.at[u, kind, i], zw_r.at[u, kind, i], (base + i, d))

    def share_x(u, j):
        i = mate(j)
        src = x_fold.at[u, pl.ds(slot_of(i) * SHARE, SHARE)]
        return copy(src, x_slot.at[u, own], dx_s.at[u, i], dx_r.at[u, own], (base + i, d))

    def share_x_in(u, j):
        i = mate(j)
        src = x_fold.at[u, pl.ds(mine, SHARE)]
        return copy(src, x_slot.at[u, i], dx_s.at[u, i], dx_r.at[u, i], (base + i, d))

    def share_gates(u, j):
        i = mate(j)
        src = gates_own.at[u, pl.ds(slot_of(i) * SHARE, SHARE)]
        return copy(src, gates_slot.at[u, own], dg_s.at[u, i], dg_r.at[u, own], (base + i, d))

    def share_gates_in(u, j):
        i = mate(j)
        src = gates_own.at[u, pl.ds(mine, SHARE)]
        return copy(src, gates_slot.at[u, i], dg_s.at[u, i], dg_r.at[u, i], (base + i, d))

    def back_d(u, j, h):
        i = mate(j)
        src = d_slot.at[u, i, pl.ds(h * PART, PART)]
        dst = d_in.at[u, pl.ds(mine + h * PART, PART)]
        return copy(src, dst, rd_s.at[u, i, h], rd_r.at[u, own, h], (base + i, d))

    def back_d_in(u, j, h):
        i = mate(j)
        src = d_slot.at[u, i, pl.ds(h * PART, PART)]
        dst = d_in.at[u, pl.ds(slot_of(i) * SHARE + h * PART, PART)]
        return copy(src, dst, rd_s.at[u, i, h], rd_r.at[u, i, h], (base + i, d))

    def back_p(u, j, h):
        i = mate(j)
        src = p_slot.at[u, i, pl.ds(h * PART, PART)]
        dst = p_in.at[u, pl.ds(mine + h * PART, PART)]
        return copy(src, dst, rp_s.at[u, i, h], rp_r.at[u, own, h], (base + i, d))

    def back_p_in(u, j, h):
        i = mate(j)
        src = p_slot.at[u, i, pl.ds(h * PART, PART)]
        dst = p_in.at[u, pl.ds(slot_of(i) * SHARE + h * PART, PART)]
        return copy(src, dst, rp_s.at[u, i, h], rp_r.at[u, i, h], (base + i, d))

    def cot_copy(r):
        src = cot.at[pl.ds(pl.multiple_of(r * 2 * TILE, 2 * TILE), 2 * TILE)]
        return copy(src, window.at[s], cot_s.at[r], cot_r.at[s], (r, d))

    def to_first(body):
        def one(r):
            @pl.when(s != r)
            def _():
                body(r)

        repeat(0, TEAM, one)

    to_first(lambda r: cot_copy(r).start())

    for kind in (0, 1):
        for j in range(1, TEAM):
            team_weights(1, j, kind).start()


    def gather_copy(u, i, at, xs, cs, kind, dev):
        ref = piece(u, i, 2 * xs + cs, kind)
        return copy(ref, ref, gat_s.at[u, i, at], gat_r.at[u, i, at], dev)

    def gather_sends(u, i):
        return [
            gather_copy(u, i, 0, x, c, 0, dev_right),
            gather_copy(u, i, 1, x, c, 1, dev_right),
            gather_copy(u, i, 2, x, c, 0, dev_left),
            gather_copy(u, i, 3, x, c, 1, dev_left),
            gather_copy(u, i, 4, left, c, 0, dev_right),
            gather_copy(u, i, 5, right, c, 1, dev_left),
        ] + [
            gather_copy(u, i, 6 + 2 * n + kind, xs, c, kind, sib)
            for n, xs in enumerate((x, left, right, far))
            for kind in (0, 1)
        ]

    def gather_recvs(u, i):
        return [
            gather_copy(u, i, 0, left, c, 0, dev_left),
            gather_copy(u, i, 1, left, c, 1, dev_left),
            gather_copy(u, i, 2, right, c, 0, dev_right),
            gather_copy(u, i, 3, right, c, 1, dev_right),
            gather_copy(u, i, 4, far, c, 0, dev_left),
            gather_copy(u, i, 5, far, c, 1, dev_right),
        ] + [
            gather_copy(u, i, 6 + 2 * n + kind, xs, 1 - c, kind, sib)
            for n, xs in enumerate((x, left, right, far))
            for kind in (0, 1)
        ]

    def gather_open(u, i):
        out = gather_sends(u, i)
        for n in (0, 3, 1, 2, 6, 7):
            out[n].start()

    def gather_close(u, i):
        out, arr = gather_sends(u, i), gather_recvs(u, i)
        arr[0].wait_recv()
        out[4].start()
        out[8].start()
        arr[3].wait_recv()
        out[5].start()
        out[11].start()
        arr[1].wait_recv()
        out[9].start()
        arr[2].wait_recv()
        out[10].start()
        arr[4].wait_recv()
        out[12].start()
        arr[5].wait_recv()
        out[13].start()
        for n in range(6, 14):
            arr[n].wait_recv()

    def gather_next(u, j):
        for kind in (0, 1):
            team_weights_in(u, j, kind).wait_recv()
        gather_open(u, mate(j))

    def gates(u):
        flat = MICRO * TILE
        pre = jnp.zeros((flat, RANK), F32)
        squares = jnp.zeros((flat, 1), F32)
        for e in range(N_DP):
            part = stash[u, :, :, e * SHARD : (e + 1) * SHARD].reshape(flat, SHARD)
            wide = part.astype(F32)
            squares = squares + jnp.sum(wide * wide, axis=1, keepdims=True)
            q, off = e // PER_PART, (e % PER_PART) * SHARD
            pre = pre + lax.dot_general(
                part, w_a[u, own, q * RANK : (q + 1) * RANK, off : off + SHARD], NT, preferred_element_type=F32
            )
        inv = lax.rsqrt(squares * (1.0 / D) + norm_epsilon)
        pre = pre * inv
        sig = 1.0 / (1.0 + jnp.exp(-pre))
        hidden = pre * sig
        turn = sig * (1.0 + pre * (1.0 - sig)) * inv
        lean = pre * inv * (1.0 / D)
        for m in range(MICRO):
            for j in range(FOLD):
                here = m * FOLD + j
                rows = slice(m * TILE, (m + 1) * TILE)
                gates_own[u, here, 0] = spread(jnp.where(group == j, turn[rows], 0.0))
                gates_own[u, here, 1] = spread(jnp.where(group == j, lean[rows], 0.0))
                hid[u, here] = spread(jnp.where(group == j, hidden[rows], 0.0)).astype(BF16)

    def give_x(u):
        for j in range(1, TEAM):
            share_x(u, j).start()

        def keep_own(k):
            x_slot[u, own, k] = x_fold[u, mine + k]

        repeat(0, SHARE, keep_own)

    def give_gates(u):
        gates(u)
        for j in range(1, TEAM):
            share_gates(u, j).start()

        def keep_own(k):
            gates_slot[u, own, k] = gates_own[u, mine + k]

        repeat(0, SHARE, keep_own)

    def take_x(u):
        for j in range(1, TEAM):
            share_x_in(u, j).wait_recv()

    def take_gates(u):
        for j in range(1, TEAM):
            share_gates_in(u, j).wait_recv()

    gather_open(1, own)
    own_weights(0)
    fold_stash(1)
    give_x(1)
    gather_close(1, own)
    give_gates(1)
    repeat(1, TEAM, lambda j: gather_next(1, j))
    fold_stash(0)

    @pl.when(first)
    def _():
        window[s] = cot[pl.ds(pl.multiple_of(s * 2 * TILE, 2 * TILE), 2 * TILE), :]

        def arrive(i):
            copy(
                cot.at[pl.ds(0, 2 * TILE)], window.at[lax.rem(s + i, N_SECTION)], cot_s.at[0],
                cot_r.at[lax.rem(s + i, N_SECTION)], sib,
            ).wait_recv()

        repeat(1, N_SECTION, arrive)

        def tile(q, at, m):
            column = (q * WIDE + at) // RANK
            start, place = column // 5 * 4, column % 5
            rows = slice(m * TILE, (m + 1) * TILE)
            value = None
            if place < 4:
                value = window[start + place, rows, :RANK].astype(F32)
            if place > 0:
                other = window[start + place - 1, rows, RANK:].astype(F32)
                value = other if value is None else value + other
            return value

        for m in range(2):
            def put(j, at, value):
                d_slot[1, 0, m * FOLD + j, :, at : at + RANK] = value

            refold(lambda q, at: tile(q, at, m), put)

    def lower_weights():
        for kind in (0, 1):
            for j in range(1, TEAM):
                team_weights(0, j, kind).start()

    def lower_inputs():
        give_x(0)

    take_x(1)
    pl.when(team >= WEIGHTS)(lower_weights)
    pl.when(team >= INPUTS)(lower_inputs)
    repeat(1, TEAM, lambda j: gather_close(1, mate(j)))
    gather_open(0, own)
    take_gates(1)

    def lower_gates():
        gather_close(0, own)
        give_gates(0)

    def lower_open():
        repeat(1, TEAM, lambda j: gather_next(0, j))

    def lower_close():
        repeat(1, TEAM, lambda j: gather_close(0, mate(j)))
        take_x(0)
        take_gates(0)

    pl.when(team >= GATES)(lower_gates)
    pl.when(team >= OPEN)(lower_open)

    pl.when(team >= LATE)(lower_close)

    def chain_copy(u, k, dev):
        place = d_slot.at[1, 0, k] if u == 1 else d_slot.at[0, TEAM - 1, k]
        return copy(d_out.at[u, k], place, ch_s.at[u, k], ch_r.at[u, k], dev)

    def block(u, i, k, incoming):
        wide = jnp.dot(incoming, w_b[u, i], preferred_element_type=F32)
        picked = jnp.where(group == 0, wide[:, :RANK], 0.0)
        for q in range(1, FOLD):
            picked = jnp.where(group == q, wide[:, q * RANK : (q + 1) * RANK], picked)
        grad_hidden = spread(picked)
        small = (grad_hidden * gates_slot[u, i, k, 0]).astype(BF16)
        p_slot[u, i, k] = small
        grad_pre = small.astype(F32)
        shift = jnp.sum(grad_pre * gates_slot[u, i, k, 1], axis=1, keepdims=True)
        diag = diagonal(grad_pre, group).astype(BF16)
        back = jnp.dot(diag, w_a[u, i], preferred_element_type=F32)
        return (incoming.astype(F32) + back - x_slot[u, i, k].astype(F32) * shift).astype(BF16)

    def walk(u, k):
        order = list(range(TEAM)) if u == 1 else list(range(TEAM))[::-1]
        value = d_slot[u, order[0], k]
        for n, i in enumerate(order):
            value = block(u, i, k, value)
            if n < TEAM - 1:
                d_slot[u, order[n + 1], k] = value
        return value

    def upper(k):
        @pl.when(team > 0)
        def _():
            chain_copy(1, k, up).wait_recv()

        out = walk(1, k)

        @pl.when(last)
        def _():
            d_slot[0, TEAM - 1, k] = out

        @pl.when(team < TEAMS - 1)
        def _():
            d_out[1, k] = out
            chain_copy(1, k, down).start()

    def give_back(u, h):
        for j in range(1, TEAM):
            back_d(u, j, h).start()
            back_p(u, j, h).start()

    def lower(k):
        @pl.when(team < TEAMS - 1)
        def _():
            chain_copy(0, k, down).wait_recv()

        out = walk(0, k)

        @pl.when(team > 0)
        def _():
            d_out[0, k] = out
            chain_copy(0, k, up).start()

        @pl.when(first & (k % PART == PART - 1) & (k < SHARE - 1))
        def _():
            give_back(0, k // PART)

    def partial(u, kind, h):
        rows = CHUNKS * TILE
        small = hid[u] if kind == 0 else p_in[u]
        right_side = d_in if kind == 0 else x_fold
        lhs = jnp.concatenate([small * mask[q][None] for q in range(FOLD)], axis=2).reshape(rows, FOLD * RANK)
        col = pl.multiple_of(h * SHARD, SHARD)
        rhs = right_side[u, :, :, pl.ds(col, SHARD)].reshape(rows, SHARD)
        return lax.dot_general(lhs, rhs, TN, preferred_element_type=F32).reshape(N_X, RANK, SHARD)

    def pair_copy(u, kind):
        return copy(pair_out.at[u, kind], pair_in.at[u, kind], pair_s.at[u, kind], pair_r.at[u, kind], sib)

    def ring_copy(u, kind, at, dev):
        return copy(ring_out.at[u, kind, at], ring_in.at[u, kind, at], ring_s.at[u, kind, at], ring_r.at[u, kind, at], dev)

    def gradients(u):
        def keep_own(k):
            d_in[u, mine + k] = d_slot[u, own, k]
            p_in[u, mine + k] = p_slot[u, own, k]

        repeat(0, SHARE, keep_own)
        for j in range(1, TEAM):
            for h in range(PARTS):
                back_d_in(u, j, h).wait_recv()
                back_p_in(u, j, h).wait_recv()
        for kind in (0, 1):
            pair_out[u, kind] = partial(u, kind, 1 - c).astype(BF16)
            pair_copy(u, kind).start()
        for kind in (0, 1):
            keep[kind] = partial(u, kind, c)
        ways = ((dev_right, right, dev_left, left), (dev_left, left, dev_right, right))
        for kind in (0, 1):
            ahead, ahead_x, behind, behind_x = ways[kind]
            pair_copy(u, kind).wait_recv()
            keep[kind] = keep[kind] + pair_in[u, kind].astype(F32)
            ring_out[u, kind, 0] = keep[kind, far].astype(BF16)
            ring_copy(u, kind, 0, ahead).start()
            ring_out[u, kind, 1] = keep[kind, behind_x].astype(BF16)
            ring_copy(u, kind, 1, behind).start()
        for kind in (0, 1):
            ahead, ahead_x, behind, behind_x = ways[kind]
            ring_copy(u, kind, 0, behind).wait_recv()
            ring_out[u, kind, 2] = (keep[kind, ahead_x] + ring_in[u, kind, 0].astype(F32)).astype(BF16)
            ring_copy(u, kind, 2, ahead).start()
        squares = jnp.zeros((1, 1), F32)
        for kind in (0, 1):
            ahead, ahead_x, behind, behind_x = ways[kind]
            ring_copy(u, kind, 1, ahead).wait_recv()
            ring_copy(u, kind, 2, behind).wait_recv()
            grad = keep[kind, x] + ring_in[u, kind, 1].astype(F32) + ring_in[u, kind, 2].astype(F32)
            squares = squares + jnp.sum(jnp.sum(grad * grad, axis=0, keepdims=True), axis=1, keepdims=True)
            if kind == 0:
                grad_b[u] = grad
            else:
                grad_a[u] = grad.T
        norm_out[...] = norm_out[...] + jnp.broadcast_to(squares, (8, 128))

    norm_out[...] = jnp.zeros((8, 128), F32)

    lag = jnp.where(team < LATE, SHARE, jnp.minimum(SHARE, LAG * (TEAMS - 1 - team)))

    def tick(t):
        upper(t)

        @pl.when(t >= lag)
        def _():
            lower(t - lag)

    repeat(0, SHARE, tick)

    def back_upper():
        repeat(0, PARTS, lambda h: give_back(1, h))

    pl.when(team < WEIGHTS)(lower_weights)
    pl.when(team < INPUTS)(lower_inputs)
    pl.when(team < GATES)(lower_gates)
    pl.when(team < OPEN)(lower_open)
    pl.when(team < LATE)(lower_close)
    pl.when(team < BACK)(back_upper)
    pl.when(team < EARLY)(lambda: gradients(1))
    repeat(SHARE - lag, SHARE, lower)
    pl.when(team >= BACK)(back_upper)
    pl.when(team > 0)(lambda: repeat(0, PARTS - 1, lambda h: give_back(0, h)))
    give_back(0, PARTS - 1)
    pl.when(team >= EARLY)(lambda: gradients(1))
    gradients(0)

    def finish(squares):
        norm = jnp.sqrt(squares)
        clip = jnp.minimum(1.0, (0.5 * math.sqrt(4 * N_SECTION * D * RANK)) / norm)[:1, :]
        total[0, 0] = norm[0, 0]
        for u in (0, 1):
            grad_a[u] = grad_a[u] * clip
            grad_b[u] = grad_b[u] * clip[:, :1]

    @pl.when(s > 0)
    def _():
        up_copy = copy(norm_out, norm_in.at[s], nrm_s, nrm_r.at[s], home)
        up_copy.start()
        copy(lane_out, tot_in, lan_s.at[0], tot_r, home).wait_recv()
        finish(tot_in[...])
        up_copy.wait_send()

    @pl.when(s == 0)
    def _():
        norm_in[0] = norm_out[...]
        repeat(1, N_SECTION, lambda i: copy(norm_out, norm_in.at[i], nrm_s, nrm_r.at[i], sib).wait_recv())
        lane_out[...] = jnp.sum(norm_in[...], axis=0)

        def share(i):
            return copy(lane_out, lane_in.at[i], lan_s.at[i], lan_r.at[i], (0, lax.rem(d + i, N_DP)))

        for i in range(1, N_DP):
            share(i).start()
        for i in range(1, N_DP):
            share(i).wait_recv()
        lane_in[0] = lane_out[...]
        value = jnp.sum(lane_in[...], axis=0)
        norm_out[...] = value
        repeat(1, N_SECTION, lambda i: copy(norm_out, tot_in, tot_s.at[i], tot_r, (i, d)).start())
        finish(value)
        repeat(1, N_SECTION, lambda i: copy(norm_out, tot_in, tot_s.at[i], tot_r, (i, d)).wait_send())
        for i in range(1, N_DP):
            share(i).wait_send()

    to_first(lambda r: cot_copy(r).wait_send())
    for u in (0, 1):
        def sent(j):
            for one in gather_sends(u, mate(j)):
                one.wait_send()

        repeat(0, TEAM, sent)
        for kind in (0, 1):
            pair_copy(u, kind).wait_send()
            for at in range(3):
                ring_copy(u, kind, at, sib).wait_send()

        def given(j):
            for kind in (0, 1):
                team_weights(u, j, kind).wait_send()
            share_x(u, j).wait_send()
            share_gates(u, j).wait_send()
            for h in range(PARTS):
                back_d(u, j, h).wait_send()
                back_p(u, j, h).wait_send()

        repeat(1, TEAM, given)

    @pl.when(team < TEAMS - 1)
    def _():
        repeat(0, SHARE, lambda k: chain_copy(1, k, down).wait_send())

    @pl.when(team > 0)
    def _():
        repeat(0, SHARE, lambda k: chain_copy(0, k, up).wait_send())


def chain(stash, cot, a_param, b_param):
    dma = pltpu.SemaphoreType.DMA
    vmem = pl.BlockSpec(memory_space=pltpu.VMEM)
    part = (2, 2, N_X, RANK, SHARD)
    own_rows = (2, CHUNKS, TILE)
    slot_rows = (2, TEAM, SHARE, TILE)
    return pl.pallas_call(
        chain_kernel,
        name="chain",
        out_shape=(
            jax.ShapeDtypeStruct((2, SHARD, RANK), F32),
            jax.ShapeDtypeStruct((2, RANK, SHARD), F32),
            jax.ShapeDtypeStruct((1, 1), F32),
        ),
        in_specs=[vmem] * 4,
        out_specs=(vmem, vmem, pl.BlockSpec(memory_space=pltpu.SMEM)),
        scratch_shapes=[
            pltpu.VMEM((2, TEAM, WIDE, FOLD * RANK), BF16),
            pltpu.VMEM((2, TEAM, FOLD * RANK, WIDE), BF16),
            pltpu.VMEM(own_rows + (WIDE,), BF16),
            pltpu.VMEM((2, CHUNKS, 2, TILE, RANK), F32),
            pltpu.VMEM(own_rows + (RANK,), BF16),
            pltpu.VMEM(own_rows + (WIDE,), BF16),
            pltpu.VMEM(own_rows + (RANK,), BF16),
            pltpu.VMEM(slot_rows + (WIDE,), BF16),
            pltpu.VMEM((2, TEAM, SHARE, 2, TILE, RANK), F32),
            pltpu.VMEM(slot_rows + (WIDE,), BF16),
            pltpu.VMEM(slot_rows + (RANK,), BF16),
            pltpu.VMEM((2, SHARE, TILE, WIDE), BF16),
            pltpu.VMEM((N_SECTION, 2 * TILE, 2 * RANK), BF16),
            pltpu.VMEM((FOLD, TILE, RANK), BF16),
            pltpu.VMEM((2, N_X, RANK, SHARD), F32),
            pltpu.VMEM(part, BF16),
            pltpu.VMEM(part, BF16),
            pltpu.VMEM((2, 2, 3, RANK, SHARD), BF16),
            pltpu.VMEM((2, 2, 3, RANK, SHARD), BF16),
            pltpu.VMEM((8, 128), F32),
            pltpu.VMEM((N_SECTION, 8, 128), F32),
            pltpu.VMEM((8, 128), F32),
            pltpu.VMEM((N_DP, 8, 128), F32),
            pltpu.VMEM((8, 128), F32),
            dma((2, 2, TEAM)), dma((2, 2, TEAM)),
            dma((2, TEAM, 14)), dma((2, TEAM, 14)),
            dma((2, TEAM)), dma((2, TEAM)),
            dma((2, TEAM)), dma((2, TEAM)),
            dma((2, TEAM, PARTS)), dma((2, TEAM, PARTS)),
            dma((2, TEAM, PARTS)), dma((2, TEAM, PARTS)),
            dma((2, SHARE)), dma((2, SHARE)),
            dma((TEAM,)), dma((N_SECTION,)),
            dma((2, 2)), dma((2, 2)),
            dma((2, 2, 3)), dma((2, 2, 3)),
            dma, dma((N_SECTION,)),
            dma((N_DP,)), dma((N_DP,)),
            dma((N_SECTION,)), dma,
        ],
        compiler_params=pltpu.CompilerParams(collective_id=0, has_side_effects=True, vmem_limit_bytes=60 << 20),
    )(stash, cot, a_param, b_param)


def adam_update(param, moment, second, scaled):
    moment_new = beta_one * moment + (1.0 - beta_one) * scaled
    second_new = beta_two * second + (1.0 - beta_two) * scaled * scaled
    param_new = param - learning_rate * moment_new / (jnp.sqrt(second_new) + adam_epsilon)
    return (param_new, moment_new, second_new)


def shards(stash, cotangent, a_param, a_moment, a_second, b_param, b_moment, b_second):
    position = lax.axis_index("section")
    flat = cotangent.reshape(MICRO * TILE, D // N_SECTION)
    cot = lax.dynamic_update_slice(
        jnp.zeros((MICRO * TILE, 2 * RANK), BF16), flat, (0, 32 * lax.rem(position, 4))
    )
    grad_a, grad_b, total = chain(stash[:, 0], cot, a_param[:, 0], b_param[:, 0])
    grad_norm = total.reshape(())
    a_new, a_moment_new, a_second_new = adam_update(a_param, a_moment, a_second, grad_a[:, None])
    b_new, b_moment_new, b_second_new = adam_update(b_param, b_moment, b_second, grad_b[:, None])
    return (a_new, a_moment_new, a_second_new, b_new, b_moment_new, b_second_new, grad_norm)


def solution(mesh):
    return jax.shard_map(
        shards,
        mesh=mesh,
        in_specs=(
            P(None, "section", None, "dp", None),
            P(None, "dp", "section"),
            P(None, "section", "dp", None),
            P(None, "section", "dp", None),
            P(None, "section", "dp", None),
            P(None, "section", None, "dp"),
            P(None, "section", None, "dp"),
            P(None, "section", None, "dp"),
        ),
        out_specs=(
            P(None, "section", "dp", None),
            P(None, "section", "dp", None),
            P(None, "section", "dp", None),
            P(None, "section", None, "dp"),
            P(None, "section", None, "dp"),
            P(None, "section", None, "dp"),
            P(),
        ),
        check_vma=False,
    )
```
